256 devices in a mesh: row: 32 (over z, x), col: 8 (over y, core).
Axes of the slice: x: 4, y: 4, z: 8, core: 2. Of those that a mesh axis runs over, the one named last changes fastest.
Arguments:
- gradient: bfloat16 [2, 8192, 16384], P(None, 'row', 'col'), may hold values from -150 to 150
- momentum: float32 [2, 8192, 16384], P(None, 'row', 'col'), may hold values from -6 to 6
- prior_input_frame: float32 [2, 8, 2048, 256], P(None, 'col', 'row'), may hold values from -6 to 6
Outputs:
- momentum_next: float32 [2, 8192, 16384], P(None, 'row', 'col')
- left_basis: float32 [2, 8192, 256], P(None, 'row')
- fresh_input_frame: float32 [2, 8, 2048, 256], P(None, 'col', 'row')
The draws below stay inside these ranges and needn't reach their ends.
All inputs are finite; a program needn't handle non-finite values.
Results may differ from the reference program's by a relative error of at most 0.0003.
Values sent between devices are 32-bit elements; how exact they have to be, the bound alone decides.
No kernel may reach another device: no remote copies, remote signals or barrier semaphores. Data moves between devices by JAX's collectives and lax.ppermute only.
A program may use at most 64 MiB of HBM per device.

```python
import math
import jax
import jax.numpy as jnp
from jax import lax

D = 8192
FF_WIN = 16384
R = 256
MATS = 2
N_COL = 8


def draw_gradient(key, part):
    key = jax.random.fold_in(key, 11)
    keys = jax.random.split(key, 3)
    ramp = jnp.exp(math.log(3.0) * jnp.arange(D, dtype=jnp.float32) / D)
    row_scale = jnp.exp(jax.random.uniform(keys[1], (MATS, D, 1), jnp.float32, 0.0, math.log(10.0))) * ramp[None, :, None]
    col_scale = jnp.exp(jax.random.uniform(keys[2], (MATS, 1, FF_WIN), jnp.float32, 0.0, math.log(10.0)))
    base = jnp.clip(jax.random.normal(keys[0], (MATS, D, FF_WIN), jnp.float32), -5.0, 5.0)
    return (base * row_scale * col_scale / 10.0).astype(jnp.bfloat16)


def shard_levels(rng, shape, shards, smallest, top_value):
    def one(position, blocks):
        steps = jax.random.uniform(jax.random.fold_in(jax.random.fold_in(rng, 6), position), (blocks,), jnp.float32, smallest / len(shards), top_value / len(shards))
        return jnp.repeat(jnp.exp(steps), shape[position] // blocks).reshape((-1,) + (1,) * (len(shape) - position - 1))

    gain = one(*shards[0])
    for cut in shards[1:]:
        gain = gain * one(*cut)
    return gain


def gaussian(stream_key, shape, spread, bound, cuts=(), kind=jnp.bfloat16):
    result = jax.random.normal(stream_key, shape, jnp.float32) * spread
    if len(cuts) > 0:
        result = shard_levels(stream_key, shape, cuts, -0.22, 0.18) * result
    return jnp.clip(result, min=-bound, max=bound).astype(kind)


def setup_inputs(seed: int = 0) -> dict:
    key_list = jax.random.split(jax.random.key(seed), 4)
    gradient = draw_gradient(jax.random.fold_in(key_list[3], 71), 0)
    momentum = gaussian(key_list[1], (MATS, D, FF_WIN), 1.0, 6.0, ((1, 32), (2, 8)), jnp.float32)
    prior_input_frame = gaussian(key_list[2], (MATS, N_COL, FF_WIN // N_COL, R), 1.0, 6.0, ((1, 8), (2, 32)), jnp.float32)
    return dict(gradient=gradient, momentum=momentum, prior_input_frame=prior_input_frame)


keep_rate = 0.95
epsilon = 1e-06

def orthonormal(product, gram):
    eye = jnp.eye(gram.shape[-1], dtype=gram.dtype)
    lower = jnp.linalg.cholesky(gram + epsilon * eye[None])
    inverse_factor = jax.scipy.linalg.solve_triangular(lower, jnp.broadcast_to(eye, gram.shape), lower=True)
    return jnp.einsum('sdq,srq->sdr', product, inverse_factor, precision=lax.Precision.HIGHEST)

def reference(gradient, momentum, prior_input_frame):
    finest_accuracy_mode = lax.Precision.HIGHEST
    buffer = momentum + gradient.astype(jnp.float32)
    basis = prior_input_frame.reshape(MATS, FF_WIN, R)
    product = jnp.einsum('sdf,sfr->sdr', buffer, basis, precision=finest_accuracy_mode)
    gram = jnp.einsum('sdr,sdq->srq', product, product, precision=finest_accuracy_mode)
    normed_output_frame = orthonormal(product, gram)
    summed = jnp.einsum('sdf,sdr->sfr', buffer, normed_output_frame, precision=finest_accuracy_mode)
    residual_feedback_term = jnp.einsum('sdr,sfr->sdf', normed_output_frame, summed, precision=finest_accuracy_mode)
    momentum_next = buffer - (1.0 - keep_rate) * residual_feedback_term
    fresh_input_frame = summed * lax.rsqrt(lax.optimization_barrier(jnp.mean(summed * summed, axis=1, keepdims=True)) + epsilon)
    return (momentum_next, normed_output_frame, fresh_input_frame.reshape(MATS, N_COL, FF_WIN // N_COL, R))
```

```python
import jax
import jax.numpy as jnp
from jax import lax
from jax.experimental import pallas as pl
from jax.experimental.pallas import tpu as pltpu
from jax.sharding import PartitionSpec as P

FF_WIN = 16384
MATS = 2
ROWS = 256
FIELDS = 2048
RANK = 256
NZ, NX, NY = 8, 4, 4
KEEP = 0.95
EPS = 1e-06
F32 = jnp.float32
BF16 = jnp.bfloat16
VMEM = pl.BlockSpec(memory_space=pltpu.VMEM)
SMEM = pl.BlockSpec(memory_space=pltpu.SMEM)
PARAMS = pltpu.CompilerParams(vmem_limit_bytes=56 * 1024 * 1024)


def sds(*shape):
    return jax.ShapeDtypeStruct(shape, F32)


def call(body, ins, outs, scratch=(), flops=0, nbytes=0):
    return pl.pallas_call(
        body,
        out_shape=outs,
        in_specs=[SMEM] + [VMEM] * (len(ins) - 1),
        out_specs=[VMEM] * len(outs),
        scratch_shapes=list(scratch),
        compiler_params=PARAMS,
        cost_estimate=pl.CostEstimate(flops=flops, bytes_accessed=nbytes, transcendentals=0),
    )(*ins)


def send_row(value, dz, dx):
    pairs = [
        (z * NX + x, (z + dz) % NZ * NX + (x + dx) % NX) for z in range(NZ) for x in range(NX)
    ]
    return lax.ppermute(value, "row", pairs)


def send_z(value, step):
    return send_row(value, step, 0)


def send_x(value, step):
    return send_row(value, 0, step)


def send_col(value, dy, dc):
    pairs = [(y * 2 + c, (y + dy) % NY * 2 + (c ^ dc)) for y in range(NY) for c in range(2)]
    return lax.ppermute(value, "col", pairs)


def ring_gather(value, size, send):
    half = size // 2
    got = {0: value}
    ahead = behind = value
    for k in range(1, half):
        ahead, behind = send(ahead, 1), send(behind, -1)
        got[size - k] = ahead
        got[k] = behind
    cut = value.shape[0] // 2
    got[half] = (send(ahead[:cut], 1), send(behind[cut:], -1))
    return [got[k] for k in range(size)]


def direct_gather(value, size, send):
    return [value if k == 0 else send(value, -k) for k in range(size)]


def ring_scatter(blocks, size, send):
    half = size // 2
    top, bottom = blocks[half]
    cut = top.shape[0]
    top, bottom = send(top, 1), send(bottom, -1)
    ahead, behind = blocks[half - 1], blocks[size - half + 1]
    ahead = jnp.concatenate([ahead[:cut] + top, ahead[cut:]], axis=0)
    behind = jnp.concatenate([behind[:cut], behind[cut:] + bottom], axis=0)
    for k in range(half - 1, 0, -1):
        ahead, behind = send(ahead, 1), send(behind, -1)
        if k > 1:
            ahead = ahead + blocks[k - 1]
            behind = behind + blocks[size - k + 1]
    return blocks[0] + ahead + behind


def direct_scatter(blocks, size, send):
    total = blocks[0]
    for k in range(1, size):
        total = total + send(blocks[k], k)
    return total


COL_STEPS = [(dy, dc) for dy in range(NY) for dc in range(2)]


def col_scatter(blocks):
    total = blocks[0]
    for (dy, dc), block in list(zip(COL_STEPS, blocks))[1:]:
        total = total + send_col(block, dy, dc)
    return total


def col_gather(value):
    return [value if (dy, dc) == (0, 0) else send_col(value, -dy, dc) for dy, dc in COL_STEPS]


def split(value):
    high = value.astype(BF16)
    return high, (value - high.astype(F32)).astype(BF16)


def dot(a, b):
    return jnp.dot(a, b, preferred_element_type=F32)


def dot3(a, b):
    return dot(a[0], b[0]) + (dot(a[0], b[1]) + dot(a[1], b[0]))


def dot_full(a, b):
    return jnp.dot(a, b, preferred_element_type=F32, precision=lax.Precision.HIGHEST)


def owner(pos_ref, k):
    dy, dc = COL_STEPS[k]
    y, c = pos_ref[2], pos_ref[3]
    return lax.rem(y + dy, NY) * 2 + (c + dc - 2 * c * dc)


def ring_at(at, k, size):
    return lax.rem(at + k, size)


def dsm(start, size, unit):
    return pl.ds(pl.multiple_of(start, unit), size)


def product_kernel(pos_ref, grad_ref, mom_ref, *refs):
    q0, q1, outs = refs[:9], refs[9:14], refs[14:22]
    q_scr, p_scr = refs[22], refs[23]
    z, x = pos_ref[0], pos_ref[1]
    pieces = [(q0[k], 0, 256, ring_at(z, k, NZ) * 256) for k in range(4)]
    pieces += [(q0[4], 0, 128, ring_at(z, 4, NZ) * 256), (q0[5], 0, 128, ring_at(z, 4, NZ) * 256 + 128)]
    pieces += [(q0[k + 1], 0, 256, ring_at(z, k, NZ) * 256) for k in range(5, 8)]
    for ref, start, size, to in pieces:
        q_scr[0, dsm(to, size, 128), :] = ref[pl.ds(start, size), :]
    for k in range(NX):
        base = ring_at(x, k, NX) * 64
        for kz in range(NZ):
            to = ring_at(z, kz, NZ) * 256 + base
            if k == 2:
                ref = q1[2] if kz < 4 else q1[3]
                block = ref[pl.ds(kz % 4 * 64, 64), :]
            else:
                block = q1[k if k < 2 else 4][pl.ds(kz * 64, 64), :]
            q_scr[1, dsm(to, 64, 64), :] = block
    for m in range(MATS):
        total = None
        for f in range(0, FIELDS, 512):
            b = mom_ref[m, :, f : f + 512] + grad_ref[m, :, f : f + 512].astype(F32)
            part = dot3(split(b), split(q_scr[m, f : f + 512, :]))
            total = part if total is None else total + part
        p_scr[m] = total
    for k in range(8):
        outs[k][...] = p_scr[:, dsm(owner(pos_ref, k) * 32, 32, 32), :]


def gram_kernel(pos_ref, *refs):
    blocks, p_ref, g_ref, t_scr = refs[:8], refs[8], refs[9], refs[10]
    for k in range(8):
        p_ref[:, dsm(owner(pos_ref, k) * 32, 32, 32), :] = blocks[k][...]
    mine = dsm(owner(pos_ref, 0) * 32, 32, 32)
    for m in range(MATS):
        t_scr[...] = p_ref[m].T
        g_ref[m] = dot_full(t_scr[mine, :], p_ref[m])


def transposed_kernel(pos_ref, p_ref, grad_ref, mom_ref, *refs):
    t0, t1, a_scr, b_scr = refs[:9], refs[9:14], refs[14], refs[15]
    z, x = pos_ref[0], pos_ref[1]
    for m in range(MATS):
        a_scr[...] = p_ref[m].T
        for kz in range(NZ):
            for kx in range(NX):
                zz, xx = ring_at(z, kz, NZ), ring_at(x, kx, NX)
                if m == 0:
                    to, at = (kz * NX + kx) * 8, (zz * NX + xx) * 8
                else:
                    to, at = (kx * NZ + kz) * 8, (xx * NZ + zz) * 8
                b_scr[m, to : to + 8, :] = a_scr[dsm(at, 8, 8), :]
        lhs = split(b_scr[m])
        for f in range(0, FIELDS, 512):
            b = mom_ref[m, :, f : f + 512] + grad_ref[m, :, f : f + 512].astype(F32)
            out = dot3(lhs, split(b))
            sizes = [32] * 4 + [16] * 2 + [32] * 3 if m == 0 else [64, 64, 32, 32, 64]
            at = 0
            for ref, size in zip(t0 if m == 0 else t1, sizes):
                ref[:, f : f + 512] = out[at : at + size]
                at += size


BLOCK = 32


def invert_blocks(blocks):
    rows = lax.broadcasted_iota(jnp.int32, (BLOCK, BLOCK), 0)
    cols = lax.broadcasted_iota(jnp.int32, (BLOCK, BLOCK), 1)
    for j in range(BLOCK):
        for m in range(len(blocks)):
            d = blocks[m]
            r = lax.rsqrt(d[j : j + 1, j : j + 1])
            row = jnp.where(cols[:1] == j, r, d[j : j + 1, :] * r)
            col = d[:, j : j + 1] * r
            new = jnp.where(cols == j, 0.0, d) - col * row
            blocks[m] = jnp.where(rows > j, new, jnp.where(rows == j, row, d))
    return [jnp.where(rows >= cols, d, 0.0) for d in blocks]


def cholesky_kernel(pos_ref, p_ref, *refs):
    gram, left_ref, x_ref, inv_ref, scr = refs[:8], refs[8], refs[9], refs[10], refs[11]
    rows = lax.broadcasted_iota(jnp.int32, (RANK, RANK), 0)
    cols = lax.broadcasted_iota(jnp.int32, (RANK, RANK), 1)
    for k in range(8):
        scr[:, dsm(owner(pos_ref, k) * 32, 32, 32), :] = gram[k][...]
    for m in range(MATS):
        scr[m] = scr[m] + jnp.where(rows == cols, EPS, 0.0)
    wide = lax.broadcasted_iota(jnp.int32, (BLOCK, RANK), 1)
    low = lax.broadcasted_iota(jnp.int32, (BLOCK, RANK), 0)
    for s in range(0, RANK, BLOCK):
        inverse = invert_blocks([scr[m, s : s + BLOCK, s : s + BLOCK] for m in range(MATS)])
        for m in range(MATS):
            panel = scr[m, s : s + BLOCK, :]
            inside = (wide >= s) & (wide < s + BLOCK)
            panel = jnp.where(inside, jnp.where(wide == low + s, 1.0, 0.0), panel)
            panel = dot_full(inverse[m], panel)
            scr[m, s : s + BLOCK, :] = panel
            if s + BLOCK < RANK:
                change = dot_full(panel.T, panel)
                below = scr[m, s + BLOCK :, :]
                cb = cols[s + BLOCK :]
                below = jnp.where((cb >= s) & (cb < s + BLOCK), 0.0, below)
                scr[m, s + BLOCK :, :] = below - change[s + BLOCK :]
    for m in range(MATS):
        inverse = jnp.where(rows >= cols, scr[m], 0.0)
        inv_ref[m] = inverse
        left = dot_full(p_ref[m], inverse.T)
        left_ref[m] = left
        x_ref[m] = (1.0 - KEEP) * dot_full(left, inverse)


def assemble(pos_ref, t0, t1, scr):
    z, x = pos_ref[0], pos_ref[1]
    for kx in range(NX):
        xx = ring_at(x, kx, NX)
        for kz in range(NZ):
            zz = ring_at(z, kz, NZ)
            if kz == 4:
                ref, at = (t0[4], kx * 8) if kx < 2 else (t0[5], (kx - 2) * 8)
            else:
                ref, at = t0[kz if kz < 4 else kz + 1], kx * 8
            scr[0, dsm((zz * NX + xx) * 8, 8, 8), :] = ref[at : at + 8, :]
            if kx == 2:
                ref, at = (t1[2], kz * 8) if kz < 4 else (t1[3], (kz - 4) * 8)
            else:
                ref, at = t1[kx if kx < 2 else 4], kz * 8
            scr[1, dsm((xx * NZ + zz) * 8, 8, 8), :] = ref[at : at + 8, :]


def right_kernel(pos_ref, inv_ref, *refs):
    t0, t1, share_ref, sq_ref, scr, flip = refs[:9], refs[9:14], refs[14], refs[15], refs[16], refs[17]
    assemble(pos_ref, t0, t1, scr)
    first = pos_ref[0] * 256 + pos_ref[1] * 64
    start = first // 128 * 128
    for m in range(MATS):
        lhs = split(inv_ref[m])
        total = jnp.zeros((RANK, 128), F32)
        for f in range(0, FIELDS, 512):
            out = dot3(lhs, split(scr[m, :, f : f + 512]))
            sq = out * out
            total += (sq[:, :128] + sq[:, 128:256]) + (sq[:, 256:384] + sq[:, 384:])
        sq_ref[m : m + 1, :] = jnp.sum(total.T, axis=0, keepdims=True)
        flip[...] = dot3(lhs, split(scr[m, :, dsm(start, 128, 128)])).T
        share_ref[m] = flip[dsm(first - start, 64, 64), :]


def feedback_kernel(pos_ref, x_ref, grad_ref, mom_ref, *refs):
    t0, t1, out_ref, scr = refs[:9], refs[9:14], refs[14], refs[15]
    assemble(pos_ref, t0, t1, scr)
    for m in range(MATS):
        lhs = split(x_ref[m])
        for f in range(0, FIELDS, 512):
            out = dot3(lhs, split(scr[m, :, f : f + 512]))
            b = mom_ref[m, :, f : f + 512] + grad_ref[m, :, f : f + 512].astype(F32)
            out_ref[m, :, f : f + 512] = b - out


def flatten(parts):
    flat = []
    for part in parts:
        flat.extend(part if isinstance(part, tuple) else [part])
    return flat


def pair(parts, half):
    return parts[:half] + [(parts[half], parts[half + 1])] + parts[half + 2 :]


def per_device(gradient, momentum, prior_input_frame):
    row, col = lax.axis_index("row"), lax.axis_index("col")
    x_at = row % NX
    pos = jnp.stack([row // NX, x_at, col // 2, col % 2]).astype(jnp.int32)
    q = prior_input_frame[:, 0]

    ordered = direct_gather(q[0], NX, send_x)
    ordered = jnp.roll(jnp.stack(ordered), x_at, axis=0).reshape(NX * 64, RANK)
    q0 = flatten(ring_gather(ordered, NZ, send_z))
    q1 = jnp.concatenate(direct_gather(q[1], NZ, send_z), axis=0)
    q1 = flatten(ring_gather(q1, NX, send_x))

    blocks = call(
        product_kernel,
        [pos, gradient, momentum] + q0 + q1,
        [sds(MATS, 32, RANK)] * 8,
        [pltpu.VMEM((MATS, FIELDS, RANK), F32), pltpu.VMEM((MATS, ROWS, RANK), F32)],
        flops=6 * MATS * ROWS * FIELDS * RANK,
        nbytes=11 << 20,
    )
    blocks = col_gather(col_scatter(blocks))
    product, gram = call(
        gram_kernel,
        [pos] + blocks,
        [sds(MATS, ROWS, RANK), sds(MATS, 32, RANK)],
        [pltpu.VMEM((RANK, ROWS), F32)],
        flops=1 << 28,
        nbytes=1 << 20,
    )

    sizes0, sizes1 = [32] * 4 + [16] * 2 + [32] * 3, [64, 64, 32, 32, 64]
    parts = call(
        transposed_kernel,
        [pos, product, gradient, momentum],
        [sds(n, FIELDS) for n in sizes0 + sizes1],
        [pltpu.VMEM((RANK, ROWS), F32), pltpu.VMEM((MATS, RANK, ROWS), F32)],
        flops=6 * MATS * ROWS * FIELDS * RANK,
        nbytes=11 << 20,
    )
    for partner in [(0, 1), (0, 2), (1, 0), (2, 0), (4, 0)]:
        pairs = [
            (z * NX + x, (z ^ partner[0]) * NX + (x ^ partner[1])) for z in range(NZ) for x in range(NX)
        ]
        gram = gram + lax.ppermute(gram, "row", pairs)
    gram = col_gather(gram)

    share0 = ring_scatter(pair(list(parts[:9]), 4), NZ, send_z)
    share1 = ring_scatter(pair(list(parts[9:]), 2), NX, send_x)
    share0 = direct_scatter([share0[k * 8 : k * 8 + 8] for k in range(NX)], NX, send_x)
    share1 = direct_scatter([share1[k * 8 : k * 8 + 8] for k in range(NZ)], NZ, send_z)
    t0 = jnp.concatenate(direct_gather(share0, NX, send_x), axis=0)
    t1 = jnp.concatenate(direct_gather(share1, NZ, send_z), axis=0)
    t0 = flatten(ring_gather(t0, NZ, send_z))
    t1 = flatten(ring_gather(t1, NX, send_x))

    left_basis, weights, inverse = call(
        cholesky_kernel,
        [pos, product] + gram,
        [sds(MATS, ROWS, RANK)] * 3,
        [pltpu.VMEM((MATS, RANK, RANK), F32)],
        flops=1 << 34,
        nbytes=2 << 20,
    )
    tall = pltpu.VMEM((MATS, RANK, FIELDS), F32)
    share, squares = call(
        right_kernel,
        [pos, inverse] + t0 + t1,
        [sds(MATS, 64, RANK), sds(MATS, RANK)],
        [tall, pltpu.VMEM((128, RANK), F32)],
        flops=6 * MATS * ROWS * FIELDS * RANK,
        nbytes=5 << 20,
    )
    total = col_gather(squares)
    total = sum(total[1:], total[0])
    (momentum_next,) = call(
        feedback_kernel,
        [pos, weights, gradient, momentum] + t0 + t1,
        [sds(MATS, ROWS, FIELDS)],
        [tall],
        flops=6 * MATS * ROWS * FIELDS * RANK,
        nbytes=15 << 20,
    )
    fresh = share * lax.rsqrt(total / FF_WIN + EPS)[:, None]
    return momentum_next, left_basis, fresh[:, None]


def solution(mesh):
    return jax.shard_map(
        per_device,
        mesh=mesh,
        in_specs=(P(None, "row", "col"), P(None, "row", "col"), P(None, "col", "row", None)),
        out_specs=(P(None, "row", "col"), P(None, "row", None), P(None, "col", "row", None)),
        check_vma=False,
    )
```

```python
import jax
import jax.numpy as jnp
from jax import lax
from jax.experimental import pallas as pl
from jax.experimental.pallas import tpu as pltpu
from jax.sharding import PartitionSpec as P

FF_WIN = 16384
MATS = 2
ROWS = 256
FIELDS = 2048
RANK = 256
NZ, NX, NY = 8, 4, 4
KEEP = 0.95
EPS = 1e-06
F32 = jnp.float32
BF16 = jnp.bfloat16
VMEM = pl.BlockSpec(memory_space=pltpu.VMEM)
SMEM = pl.BlockSpec(memory_space=pltpu.SMEM)
PARAMS = pltpu.CompilerParams(vmem_limit_bytes=56 * 1024 * 1024)


def sds(*shape):
    return jax.ShapeDtypeStruct(shape, F32)


def call(body, ins, outs, scratch=(), flops=0, nbytes=0):
    return pl.pallas_call(
        body,
        out_shape=outs,
        in_specs=[SMEM] + [VMEM] * (len(ins) - 1),
        out_specs=[VMEM] * len(outs),
        scratch_shapes=list(scratch),
        compiler_params=PARAMS,
        cost_estimate=pl.CostEstimate(flops=flops, bytes_accessed=nbytes, transcendentals=0),
    )(*ins)


def send_row(value, dz, dx):
    pairs = [
        (z * NX + x, (z + dz) % NZ * NX + (x + dx) % NX) for z in range(NZ) for x in range(NX)
    ]
    return lax.ppermute(value, "row", pairs)


def send_z(value, step):
    return send_row(value, step, 0)


def send_x(value, step):
    return send_row(value, 0, step)


def ring_gather(value, size, send):
    half = size // 2
    got = {0: value}
    ahead = behind = value
    for k in range(1, half):
        ahead, behind = send(ahead, 1), send(behind, -1)
        got[size - k] = ahead
        got[k] = behind
    cut = value.shape[0] // 2
    got[half] = (send(ahead[:cut], 1), send(behind[cut:], -1))
    return [got[k] for k in range(size)]


def exchange(blocks, axis, groups=None):
    return lax.all_to_all(blocks, axis, 0, 0, axis_index_groups=groups, tiled=True)


def spread(value, size, axis, groups=None):
    return exchange(jnp.broadcast_to(value[None], (size,) + value.shape), axis, groups)


X_GROUPS = [[z * NX + x for x in range(NX)] for z in range(NZ)]
Z_GROUPS = [[z * NX + x for z in range(NZ)] for x in range(NX)]


def ring_scatter(blocks, size, send):
    half = size // 2
    top, bottom = blocks[half]
    cut = top.shape[0]
    top, bottom = send(top, 1), send(bottom, -1)
    ahead, behind = blocks[half - 1], blocks[size - half + 1]
    ahead = jnp.concatenate([ahead[:cut] + top, ahead[cut:]], axis=0)
    behind = jnp.concatenate([behind[:cut], behind[cut:] + bottom], axis=0)
    for k in range(half - 1, 0, -1):
        ahead, behind = send(ahead, 1), send(behind, -1)
        if k > 1:
            ahead = ahead + blocks[k - 1]
            behind = behind + blocks[size - k + 1]
    return blocks[0] + ahead + behind


def split(value):
    high = value.astype(BF16)
    return high, (value - high.astype(F32)).astype(BF16)


def dot(a, b):
    return jnp.dot(a, b, preferred_element_type=F32)


def dot3(a, b):
    return dot(a[0], b[0]) + (dot(a[0], b[1]) + dot(a[1], b[0]))


def dot_full(a, b):
    return jnp.dot(a, b, preferred_element_type=F32, precision=lax.Precision.HIGHEST)


def ring_at(at, k, size):
    return lax.rem(at + k, size)


def dsm(start, size, unit):
    return pl.ds(pl.multiple_of(start, unit), size)


def product_kernel(pos_ref, grad_ref, mom_ref, *refs):
    q0, q1, out, q_scr = refs[:9], refs[9:14], refs[14], refs[15]
    z, x = pos_ref[0], pos_ref[1]
    pieces = [(q0[k], 0, 256, ring_at(z, k, NZ) * 256) for k in range(4)]
    pieces += [(q0[4], 0, 128, ring_at(z, 4, NZ) * 256), (q0[5], 0, 128, ring_at(z, 4, NZ) * 256 + 128)]
    pieces += [(q0[k + 1], 0, 256, ring_at(z, k, NZ) * 256) for k in range(5, 8)]
    for ref, start, size, to in pieces:
        q_scr[0, dsm(to, size, 128), :] = ref[pl.ds(start, size), :]
    for k in range(NX):
        base = ring_at(x, k, NX) * 64
        for kz in range(NZ):
            to = kz * 256 + base
            if k == 2:
                ref = q1[2] if kz < 4 else q1[3]
                block = ref[pl.ds(kz % 4 * 64, 64), :]
            else:
                block = q1[k if k < 2 else 4][pl.ds(kz * 64, 64), :]
            q_scr[1, dsm(to, 64, 64), :] = block
    for m in range(MATS):
        total = None
        for f in range(0, FIELDS, 512):
            b = mom_ref[m, :, f : f + 512] + grad_ref[m, :, f : f + 512].astype(F32)
            part = dot3(split(b), split(q_scr[m, f : f + 512, :]))
            total = part if total is None else total + part
        for k in range(8):
            out[k, m] = total[k * 32 : k * 32 + 32]


def gram_kernel(pos_ref, *refs):
    blocks, p_ref, g_ref = refs
    for k in range(8):
        p_ref[:, k * 32 : k * 32 + 32, :] = blocks[k]
    for m in range(MATS):
        g_ref[m] = dot_full(p_ref[m].T, p_ref[m])


def transposed_kernel(pos_ref, p_ref, grad_ref, mom_ref, *refs):
    t0, t1, a_scr, b_scr = refs[:9], refs[9:14], refs[14], refs[15]
    z, x = pos_ref[0], pos_ref[1]
    for m in range(MATS):
        a_scr[...] = p_ref[m].T
        for kz in range(NZ):
            for kx in range(NX):
                zz, xx = ring_at(z, kz, NZ), ring_at(x, kx, NX)
                if m == 0:
                    to, at = (kz * NX + kx) * 8, (zz * NX + kx) * 8
                else:
                    to, at = (kx * NZ + kz) * 8, (xx * NZ + kz) * 8
                b_scr[m, to : to + 8, :] = a_scr[dsm(at, 8, 8), :]
        lhs = split(b_scr[m])
        for f in range(0, FIELDS, 512):
            b = mom_ref[m, :, f : f + 512] + grad_ref[m, :, f : f + 512].astype(F32)
            out = dot3(lhs, split(b))
            sizes = [32] * 4 + [16] * 2 + [32] * 3 if m == 0 else [64, 64, 32, 32, 64]
            at = 0
            for ref, size in zip(t0 if m == 0 else t1, sizes):
                ref[:, f : f + 512] = out[at : at + size]
                at += size


BLOCK = 32


def invert_blocks(blocks):
    rows = lax.broadcasted_iota(jnp.int32, (BLOCK, BLOCK), 0)
    cols = lax.broadcasted_iota(jnp.int32, (BLOCK, BLOCK), 1)
    for j in range(BLOCK):
        for m in range(len(blocks)):
            d = blocks[m]
            r = lax.rsqrt(d[j : j + 1, j : j + 1])
            row = jnp.where(cols[:1] == j, r, d[j : j + 1, :] * r)
            col = d[:, j : j + 1] * r
            new = jnp.where(cols == j, 0.0, d) - col * row
            blocks[m] = jnp.where(rows > j, new, jnp.where(rows == j, row, d))
    return [jnp.where(rows >= cols, d, 0.0) for d in blocks]


def cholesky_kernel(pos_ref, p_ref, *refs):
    gram, left_ref, x_ref, inv_ref, scr = refs
    rows = lax.broadcasted_iota(jnp.int32, (RANK, RANK), 0)
    cols = lax.broadcasted_iota(jnp.int32, (RANK, RANK), 1)
    for m in range(MATS):
        scr[m] = gram[m] + jnp.where(rows == cols, EPS, 0.0)
    wide = lax.broadcasted_iota(jnp.int32, (BLOCK, RANK), 1)
    low = lax.broadcasted_iota(jnp.int32, (BLOCK, RANK), 0)
    for s in range(0, RANK, BLOCK):
        inverse = invert_blocks([scr[m, s : s + BLOCK, s : s + BLOCK] for m in range(MATS)])
        for m in range(MATS):
            panel = scr[m, s : s + BLOCK, :]
            inside = (wide >= s) & (wide < s + BLOCK)
            panel = jnp.where(inside, jnp.where(wide == low + s, 1.0, 0.0), panel)
            panel = dot_full(inverse[m], panel)
            scr[m, s : s + BLOCK, :] = panel
            if s + BLOCK < RANK:
                change = dot_full(panel.T, panel)
                below = scr[m, s + BLOCK :, :]
                cb = cols[s + BLOCK :]
                below = jnp.where((cb >= s) & (cb < s + BLOCK), 0.0, below)
                scr[m, s + BLOCK :, :] = below - change[s + BLOCK :]
    for m in range(MATS):
        inverse = jnp.where(rows >= cols, scr[m], 0.0)
        inv_ref[m] = inverse
        left = dot_full(p_ref[m], inverse.T)
        left_ref[m] = left
        x_ref[m] = (1.0 - KEEP) * dot_full(left, inverse)


def assemble(pos_ref, t0, t1, scr):
    z, x = pos_ref[0], pos_ref[1]
    for kx in range(NX):
        xx = ring_at(x, kx, NX)
        for kz in range(NZ):
            zz = ring_at(z, kz, NZ)
            if kz == 4:
                ref, at = (t0[4], kx * 8) if kx < 2 else (t0[5], (kx - 2) * 8)
            else:
                ref, at = t0[kz if kz < 4 else kz + 1], kx * 8
            scr[0, dsm((zz * NX + kx) * 8, 8, 8), :] = ref[at : at + 8, :]
            if kx == 2:
                ref, at = (t1[2], kz * 8) if kz < 4 else (t1[3], (kz - 4) * 8)
            else:
                ref, at = t1[kx if kx < 2 else 4], kz * 8
            scr[1, dsm((xx * NZ + kz) * 8, 8, 8), :] = ref[at : at + 8, :]


def right_kernel(pos_ref, inv_ref, *refs):
    t0, t1, share_ref, sq_ref, scr, flip = refs[:9], refs[9:14], refs[14], refs[15], refs[16], refs[17]
    assemble(pos_ref, t0, t1, scr)
    first = pos_ref[0] * 256 + pos_ref[1] * 64
    start = first // 128 * 128
    for m in range(MATS):
        lhs = split(inv_ref[m])
        total = jnp.zeros((RANK, 128), F32)
        for f in range(0, FIELDS, 512):
            out = dot3(lhs, split(scr[m, :, f : f + 512]))
            sq = out * out
            total += (sq[:, :128] + sq[:, 128:256]) + (sq[:, 256:384] + sq[:, 384:])
        sq_ref[m : m + 1, :] = jnp.sum(total.T, axis=0, keepdims=True)
        flip[...] = dot3(lhs, split(scr[m, :, dsm(start, 128, 128)])).T
        share_ref[m] = flip[dsm(first - start, 64, 64), :]


def feedback_kernel(pos_ref, x_ref, grad_ref, mom_ref, *refs):
    t0, t1, out_ref, scr = refs[:9], refs[9:14], refs[14], refs[15]
    assemble(pos_ref, t0, t1, scr)
    for m in range(MATS):
        lhs = split(x_ref[m])
        for f in range(0, FIELDS, 512):
            out = dot3(lhs, split(scr[m, :, f : f + 512]))
            b = mom_ref[m, :, f : f + 512] + grad_ref[m, :, f : f + 512].astype(F32)
            out_ref[m, :, f : f + 512] = b - out


def flatten(parts):
    flat = []
    for part in parts:
        flat.extend(part if isinstance(part, tuple) else [part])
    return flat


def pair(parts, half):
    return parts[:half] + [(parts[half], parts[half + 1])] + parts[half + 2 :]


def per_device(gradient, momentum, prior_input_frame):
    row, col = lax.axis_index("row"), lax.axis_index("col")
    x_at = row % NX
    pos = jnp.stack([row // NX, x_at, col // 2, col % 2]).astype(jnp.int32)
    q = prior_input_frame[:, 0]

    q0 = spread(q[0], NX, "row", X_GROUPS).reshape(NX * 64, RANK)
    q1 = spread(q[1], NZ, "row", Z_GROUPS).reshape(NZ * 64, RANK)
    q0 = flatten(ring_gather(q0, NZ, send_z))
    q1 = flatten(ring_gather(q1, NX, send_x))

    (blocks,) = call(
        product_kernel,
        [pos, gradient, momentum] + q0 + q1,
        [sds(8, MATS, 32, RANK)],
        [pltpu.VMEM((MATS, FIELDS, RANK), F32)],
        flops=6 * MATS * ROWS * FIELDS * RANK,
        nbytes=11 << 20,
    )
    blocks = spread(jnp.sum(exchange(blocks, "col"), axis=0), 8, "col")
    product, gram = call(
        gram_kernel,
        [pos, blocks],
        [sds(MATS, ROWS, RANK), sds(MATS, RANK, RANK)],
        flops=1 << 28,
        nbytes=1 << 20,
    )

    sizes0, sizes1 = [32] * 4 + [16] * 2 + [32] * 3, [64, 64, 32, 32, 64]
    parts = call(
        transposed_kernel,
        [pos, product, gradient, momentum],
        [sds(n, FIELDS) for n in sizes0 + sizes1],
        [pltpu.VMEM((RANK, ROWS), F32), pltpu.VMEM((MATS, RANK, ROWS), F32)],
        flops=6 * MATS * ROWS * FIELDS * RANK,
        nbytes=11 << 20,
    )
    gram = exchange(gram.reshape(32, 16, RANK), "row")
    gram = spread(jnp.sum(gram, axis=0), 32, "row").reshape(MATS, RANK, RANK)

    share0 = ring_scatter(pair(list(parts[:9]), 4), NZ, send_z)
    share1 = ring_scatter(pair(list(parts[9:]), 2), NX, send_x)
    share0 = jnp.sum(exchange(share0.reshape(NX, 8, FIELDS), "row", X_GROUPS), axis=0)
    share1 = jnp.sum(exchange(share1.reshape(NZ, 8, FIELDS), "row", Z_GROUPS), axis=0)
    t0 = spread(share0, NX, "row", X_GROUPS).reshape(NX * 8, FIELDS)
    t1 = spread(share1, NZ, "row", Z_GROUPS).reshape(NZ * 8, FIELDS)
    t0 = flatten(ring_gather(t0, NZ, send_z))
    t1 = flatten(ring_gather(t1, NX, send_x))

    left_basis, weights, inverse = call(
        cholesky_kernel,
        [pos, product, gram],
        [sds(MATS, ROWS, RANK)] * 3,
        [pltpu.VMEM((MATS, RANK, RANK), F32)],
        flops=1 << 34,
        nbytes=2 << 20,
    )
    tall = pltpu.VMEM((MATS, RANK, FIELDS), F32)
    share, squares = call(
        right_kernel,
        [pos, inverse] + t0 + t1,
        [sds(MATS, 64, RANK), sds(MATS, RANK)],
        [tall, pltpu.VMEM((128, RANK), F32)],
        flops=6 * MATS * ROWS * FIELDS * RANK,
        nbytes=5 << 20,
    )
    total = jnp.sum(spread(squares, 8, "col"), axis=0)
    (momentum_next,) = call(
        feedback_kernel,
        [pos, weights, gradient, momentum] + t0 + t1,
        [sds(MATS, ROWS, FIELDS)],
        [tall],
        flops=6 * MATS * ROWS * FIELDS * RANK,
        nbytes=15 << 20,
    )
    fresh = share * lax.rsqrt(total / FF_WIN + EPS)[:, None]
    return momentum_next, left_basis, fresh[:, None]


def solution(mesh):
    return jax.shard_map(
        per_device,
        mesh=mesh,
        in_specs=(P(None, "row", "col"), P(None, "row", "col"), P(None, "col", "row", None)),
        out_specs=(P(None, "row", "col"), P(None, "row", None), P(None, "col", "row", None)),
        check_vma=False,
    )
```

```python
import jax
import jax.numpy as jnp
from jax import lax
from jax.experimental import pallas as pl
from jax.experimental.pallas import tpu as pltpu
from jax.sharding import PartitionSpec as P

FF_WIN = 16384
MATS = 2
ROWS = 256
FIELDS = 2048
RANK = 256
NZ, NX, NY = 8, 4, 4
KEEP = 0.95
EPS = 1e-06
F32 = jnp.float32
BF16 = jnp.bfloat16
VMEM = pl.BlockSpec(memory_space=pltpu.VMEM)
SMEM = pl.BlockSpec(memory_space=pltpu.SMEM)
PARAMS = pltpu.CompilerParams(vmem_limit_bytes=56 * 1024 * 1024)


def sds(*shape):
    return jax.ShapeDtypeStruct(shape, F32)


def call(body, ins, outs, scratch=(), flops=0, nbytes=0):
    return pl.pallas_call(
        body,
        out_shape=outs,
        in_specs=[SMEM] + [VMEM] * (len(ins) - 1),
        out_specs=[VMEM] * len(outs),
        scratch_shapes=list(scratch),
        compiler_params=PARAMS,
        cost_estimate=pl.CostEstimate(flops=flops, bytes_accessed=nbytes, transcendentals=0),
    )(*ins)


def send_row(value, dz, dx):
    pairs = [
        (z * NX + x, (z + dz) % NZ * NX + (x + dx) % NX) for z in range(NZ) for x in range(NX)
    ]
    return lax.ppermute(value, "row", pairs)


def send_z(value, step):
    return send_row(value, step, 0)


def send_x(value, step):
    return send_row(value, 0, step)


def send_y(value, step):
    pairs = [(y * 2 + c, (y + step) % NY * 2 + c) for y in range(NY) for c in range(2)]
    return lax.ppermute(value, "col", pairs)


def send_core(value):
    return lax.ppermute(value, "col", [(k, k ^ 1) for k in range(2 * NY)])


def ring_gather_whole(value, size, send):
    got = {0: value}
    ahead = behind = value
    for k in range(1, size // 2 + 1):
        ahead = send(ahead, 1)
        got[size - k] = ahead
        if k < size // 2:
            behind = send(behind, -1)
            got[k] = behind
    return [got[k] for k in range(size)]


def ring_scatter_whole(blocks, size, send):
    half = size // 2
    ahead, behind = send(blocks[half], 1), None
    for k in range(half - 1, 0, -1):
        ahead = send(ahead + blocks[k], 1)
        part = blocks[size - k]
        behind = send(part if behind is None else behind + part, -1)
    return blocks[0] + ahead + behind


def ring_gather(value, size, send):
    half = size // 2
    got = {0: value}
    ahead = behind = value
    for k in range(1, half):
        ahead, behind = send(ahead, 1), send(behind, -1)
        got[size - k] = ahead
        got[k] = behind
    cut = value.shape[0] // 2
    got[half] = (send(ahead[:cut], 1), send(behind[cut:], -1))
    return [got[k] for k in range(size)]


def exchange(blocks, axis, groups=None):
    return lax.all_to_all(blocks, axis, 0, 0, axis_index_groups=groups, tiled=True)


def spread(value, size, axis, groups=None):
    return exchange(jnp.broadcast_to(value[None], (size,) + value.shape), axis, groups)


Z_GROUPS = [[z * NX + x for z in range(NZ)] for x in range(NX)]


def ring_scatter(blocks, size, send):
    half = size // 2
    top, bottom = blocks[half]
    cut = top.shape[0]
    top, bottom = send(top, 1), send(bottom, -1)
    ahead, behind = blocks[half - 1], blocks[size - half + 1]
    ahead = jnp.concatenate([ahead[:cut] + top, ahead[cut:]], axis=0)
    behind = jnp.concatenate([behind[:cut], behind[cut:] + bottom], axis=0)
    for k in range(half - 1, 0, -1):
        ahead, behind = send(ahead, 1), send(behind, -1)
        if k > 1:
            ahead = ahead + blocks[k - 1]
            behind = behind + blocks[size - k + 1]
    return blocks[0] + ahead + behind


def split(value):
    high = value.astype(BF16)
    return high, (value - high.astype(F32)).astype(BF16)


def dot(a, b):
    return jnp.dot(a, b, preferred_element_type=F32)


def dot3(a, b):
    return dot(a[0], b[0]) + (dot(a[0], b[1]) + dot(a[1], b[0]))


def dot_full(a, b):
    return jnp.dot(a, b, preferred_element_type=F32, precision=lax.Precision.HIGHEST)


def ring_at(at, k, size):
    return lax.rem(at + k, size)


def dsm(start, size, unit):
    return pl.ds(pl.multiple_of(start, unit), size)


def product_kernel(pos_ref, grad_ref, mom_ref, *refs):
    q0, q1, mine, other, q_scr, p_scr = refs[:8], refs[8], refs[9], refs[10], refs[11], refs[12]
    z, y, c = pos_ref[0], pos_ref[2], pos_ref[3]
    for k in range(NZ):
        q_scr[dsm(ring_at(z, k, NZ) * 256, 256, 256), :] = q0[k][...]
    for m in range(MATS):
        q = q1 if m else q_scr
        total = None
        for f in range(0, FIELDS, 512):
            b = mom_ref[m, :, f : f + 512] + grad_ref[m, :, f : f + 512].astype(F32)
            part = dot3(split(b), split(q[f : f + 512, :]))
            total = part if total is None else total + part
        p_scr[m] = total
    for k in range(NY):
        at = ring_at(y, k, NY) * 32
        mine[k] = p_scr[:, dsm(c * 128 + at, 32, 32), :]
        other[k] = p_scr[:, dsm(128 - c * 128 + at, 32, 32), :]


def gram_kernel(pos_ref, mine, other, p_ref, g_ref):
    y, c = pos_ref[2], pos_ref[3]
    for k in range(NY):
        at = ring_at(y, k, NY) * 32
        p_ref[:, dsm(c * 128 + at, 32, 32), :] = mine[k]
        p_ref[:, dsm(128 - c * 128 + at, 32, 32), :] = other[k]
    for m in range(MATS):
        g_ref[m] = dot_full(p_ref[m].T, p_ref[m])


def transposed_kernel(pos_ref, p_ref, grad_ref, mom_ref, *refs):
    t0, t1, a_scr, b_scr = refs[:8], refs[8:13], refs[13], refs[14]
    z, x = pos_ref[0], pos_ref[1]
    for m in range(MATS):
        a_scr[...] = p_ref[m].T
        for kz in range(NZ):
            for kx in range(NX):
                zz, xx = ring_at(z, kz, NZ), ring_at(x, kx, NX)
                if m == 0:
                    to, at = (kz * NX + kx) * 8, (zz * NX + xx) * 8
                else:
                    to, at = (kx * NZ + kz) * 8, (xx * NZ + kz) * 8
                b_scr[m, to : to + 8, :] = a_scr[dsm(at, 8, 8), :]
        lhs = split(b_scr[m])
        for f in range(0, FIELDS, 512):
            b = mom_ref[m, :, f : f + 512] + grad_ref[m, :, f : f + 512].astype(F32)
            out = dot3(lhs, split(b))
            sizes = [32] * 8 if m == 0 else [64, 64, 32, 32, 64]
            at = 0
            for ref, size in zip(t0 if m == 0 else t1, sizes):
                ref[:, f : f + 512] = out[at : at + size]
                at += size


BLOCK = 64


def invert_blocks(pair):
    shape = (8, 2 * BLOCK)
    lane = lax.broadcasted_iota(jnp.int32, shape, 1)
    sub = lax.broadcasted_iota(jnp.int32, shape, 0)
    first = lane < BLOCK
    at = lane % BLOCK

    def lanes(group, j):
        left = jnp.broadcast_to(group[:, j : j + 1], shape)
        return jnp.where(first, left, jnp.broadcast_to(group[:, BLOCK + j : BLOCK + j + 1], shape))

    groups = [pair[g : g + 8, :] for g in range(0, BLOCK, 8)]
    done = []
    for g in range(BLOCK // 8):
        scale = jnp.ones(shape, F32)
        for i in range(0, 8, 2):
            j = g * 8 + i
            here = groups[g]
            x, y = lanes(here, j), lanes(here, j + 1)
            a = jnp.broadcast_to(x[i : i + 1], shape)
            b = jnp.broadcast_to(x[i + 1 : i + 2], shape)
            c = jnp.broadcast_to(y[i + 1 : i + 2], shape)
            over_a = 1.0 / a
            det = a * c - b * b
            over_det = 1.0 / det
            row_j = jnp.broadcast_to(here[i : i + 1], shape)
            row_k = jnp.broadcast_to(here[i + 1 : i + 2], shape)
            in_j, in_k = at == j, at == j + 1
            pivots = in_j | in_k
            row_j = jnp.where(in_j, 1.0, jnp.where(in_k, 0.0, row_j))
            row_k = jnp.where(in_k, 1.0, jnp.where(in_j, 0.0, row_k)) - (b * over_a) * row_j
            for h in range(g, BLOCK // 8):
                if h > g:
                    x, y = lanes(groups[h], j), lanes(groups[h], j + 1)
                u = x * over_a
                v = (a * y - b * x) * over_det
                new = jnp.where(pivots, 0.0, groups[h]) - u * row_j - v * row_k
                if h == g:
                    new = jnp.where(sub > i + 1, new, here)
                    new = jnp.where(sub == i, row_j, jnp.where(sub == i + 1, row_k, new))
                groups[h] = new
            scale = jnp.where(sub == i, lax.rsqrt(a), scale)
            scale = jnp.where(sub == i + 1, lax.rsqrt(det * over_a), scale)
        done.append(jnp.where(sub + g * 8 >= at, groups[g] * scale, 0.0))
    packed = jnp.concatenate(done, axis=0)
    return [packed[:, :BLOCK], packed[:, BLOCK:]]


def cholesky_kernel(pos_ref, p_ref, *refs):
    gram, left_ref, x_ref, inv_ref, scr = refs
    rows = lax.broadcasted_iota(jnp.int32, (RANK, RANK), 0)
    cols = lax.broadcasted_iota(jnp.int32, (RANK, RANK), 1)
    for m in range(MATS):
        scr[m] = gram[m] + jnp.where(rows == cols, EPS, 0.0)
    wide = lax.broadcasted_iota(jnp.int32, (BLOCK, RANK), 1)
    low = lax.broadcasted_iota(jnp.int32, (BLOCK, RANK), 0)
    for s in range(0, RANK, BLOCK):
        e = s + BLOCK
        inverse = invert_blocks(jnp.concatenate([scr[m, s:e, s:e] for m in range(MATS)], axis=1))
        for m in range(MATS):
            panel = scr[m, s : s + BLOCK, :]
            inside = (wide >= s) & (wide < s + BLOCK)
            panel = jnp.where(inside, jnp.where(wide == low + s, 1.0, 0.0), panel)
            panel = dot_full(inverse[m], panel)
            scr[m, s : s + BLOCK, :] = panel
            if e < RANK:
                low_edge = e // 128 * 128
                change = dot_full(panel[:, low_edge:].T, panel)
                below = jnp.where((cols[e:] >= s) & (cols[e:] < e), 0.0, scr[m, e:, :])
                scr[m, e:, :] = below - change[e - low_edge :]
    for m in range(MATS):
        inverse = jnp.where(rows >= cols, scr[m], 0.0)
        inv_ref[m] = inverse
        left = dot3(split(p_ref[m]), split(inverse.T))
        left_ref[m] = left
        x_ref[m] = (1.0 - KEEP) * dot3(split(left), split(inverse))


def assemble(pos_ref, t0, t1, scr):
    x = pos_ref[1]
    scr[0] = t0[...]
    for kx in range(NX):
        start = ring_at(x, kx, NX) * 64
        if kx == 2:
            scr[1, dsm(start, 32, 32), :] = t1[2][...]
            scr[1, dsm(start + 32, 32, 32), :] = t1[3][...]
        else:
            scr[1, dsm(start, 64, 64), :] = t1[kx if kx < 2 else 4][...]


def right_kernel(pos_ref, inv_ref, *refs):
    t0, t1, share_ref, sq_ref, scr, flip = refs[0], refs[1:6], refs[6], refs[7], refs[8], refs[9]
    assemble(pos_ref, t0, t1, scr)
    first = pos_ref[0] * 256 + pos_ref[1] * 64
    start = first // 128 * 128
    for m in range(MATS):
        lhs = split(inv_ref[m])
        total = jnp.zeros((RANK, 128), F32)
        for f in range(0, FIELDS, 512):
            out = dot3(lhs, split(scr[m, :, f : f + 512]))
            sq = out * out
            total += (sq[:, :128] + sq[:, 128:256]) + (sq[:, 256:384] + sq[:, 384:])
        sq_ref[m : m + 1, :] = jnp.sum(total.T, axis=0, keepdims=True)
        flip[...] = dot3(lhs, split(scr[m, :, dsm(start, 128, 128)])).T
        share_ref[m] = flip[dsm(first - start, 64, 64), :]


def feedback_kernel(pos_ref, x_ref, grad_ref, mom_ref, *refs):
    t0, t1, out_ref, scr = refs[0], refs[1:6], refs[6], refs[7]
    assemble(pos_ref, t0, t1, scr)
    for m in range(MATS):
        lhs = split(x_ref[m])
        for f in range(0, FIELDS, 512):
            out = dot3(lhs, split(scr[m, :, f : f + 512]))
            b = mom_ref[m, :, f : f + 512] + grad_ref[m, :, f : f + 512].astype(F32)
            out_ref[m, :, f : f + 512] = b - out


def flatten(parts):
    flat = []
    for part in parts:
        flat.extend(part if isinstance(part, tuple) else [part])
    return flat


def pair(parts, half):
    return parts[:half] + [(parts[half], parts[half + 1])] + parts[half + 2 :]


def per_device(gradient, momentum, prior_input_frame):
    row, col = lax.axis_index("row"), lax.axis_index("col")
    x_at = row % NX
    pos = jnp.stack([row // NX, x_at, col // 2, col % 2]).astype(jnp.int32)
    q = prior_input_frame[:, 0]

    q1 = lax.all_gather(q[1], "row", axis=0, tiled=True)
    q0 = jnp.stack([q[0]] + [send_x(q[0], -k) for k in range(1, NX)])
    q0 = jnp.roll(q0, x_at, axis=0).reshape(NX * 64, RANK)
    q0 = ring_gather_whole(q0, NZ, send_z)

    mine, other = call(
        product_kernel,
        [pos, gradient, momentum] + q0 + [q1],
        [sds(NY, MATS, 32, RANK)] * 2,
        [pltpu.VMEM((FIELDS, RANK), F32), pltpu.VMEM((MATS, ROWS, RANK), F32)],
        flops=6 * MATS * ROWS * FIELDS * RANK,
        nbytes=11 << 20,
    )
    other = send_core(other)
    mine = [mine[k] + other[k] for k in range(NY)]
    share = mine[0] + sum(send_y(mine[k], k) for k in range(1, NY))
    mine = jnp.stack([share] + [send_y(share, -k) for k in range(1, NY)])
    other = send_core(mine)
    product, gram = call(
        gram_kernel,
        [pos, mine, other],
        [sds(MATS, ROWS, RANK), sds(MATS, RANK, RANK)],
        flops=1 << 28,
        nbytes=1 << 20,
    )

    sizes0, sizes1 = [32] * 8, [64, 64, 32, 32, 64]
    parts = call(
        transposed_kernel,
        [pos, product, gradient, momentum],
        [sds(n, FIELDS) for n in sizes0 + sizes1],
        [pltpu.VMEM((RANK, ROWS), F32), pltpu.VMEM((MATS, RANK, ROWS), F32)],
        flops=6 * MATS * ROWS * FIELDS * RANK,
        nbytes=11 << 20,
    )
    gram = exchange(gram.reshape(32, 16, RANK), "row")
    gram = spread(jnp.sum(gram, axis=0), 32, "row").reshape(MATS, RANK, RANK)

    share0 = ring_scatter_whole(list(parts[:8]), NZ, send_z)
    share1 = ring_scatter(pair(list(parts[8:]), 2), NX, send_x)
    pieces = [share0[k * 8 : k * 8 + 8] for k in range(NX)]
    share0 = pieces[0] + sum(send_x(pieces[k], k) for k in range(1, NX))
    t0 = lax.all_gather(share0, "row", axis=0, tiled=True)
    share1 = jnp.sum(exchange(share1.reshape(NZ, 8, FIELDS), "row", Z_GROUPS), axis=0)
    t1 = spread(share1, NZ, "row", Z_GROUPS).reshape(NZ * 8, FIELDS)
    t1 = flatten(ring_gather(t1, NX, send_x))

    left_basis, weights, inverse = call(
        cholesky_kernel,
        [pos, product, gram],
        [sds(MATS, ROWS, RANK)] * 3,
        [pltpu.VMEM((MATS, RANK, RANK), F32)],
        flops=1 << 34,
        nbytes=2 << 20,
    )
    tall = pltpu.VMEM((MATS, RANK, FIELDS), F32)
    share, squares = call(
        right_kernel,
        [pos, inverse, t0] + t1,
        [sds(MATS, 64, RANK), sds(MATS, RANK)],
        [tall, pltpu.VMEM((128, RANK), F32)],
        flops=6 * MATS * ROWS * FIELDS * RANK,
        nbytes=5 << 20,
    )
    total = jnp.sum(spread(squares, 8, "col"), axis=0)
    (momentum_next,) = call(
        feedback_kernel,
        [pos, weights, gradient, momentum, t0] + t1,
        [sds(MATS, ROWS, FIELDS)],
        [tall],
        flops=6 * MATS * ROWS * FIELDS * RANK,
        nbytes=15 << 20,
    )
    fresh = share * lax.rsqrt(total / FF_WIN + EPS)[:, None]
    return momentum_next, left_basis, fresh[:, None]


def solution(mesh):
    return jax.shard_map(
        per_device,
        mesh=mesh,
        in_specs=(P(None, "row", "col"), P(None, "row", "col"), P(None, "col", "row", None)),
        out_specs=(P(None, "row", "col"), P(None, "row", None), P(None, "col", "row", None)),
        check_vma=False,
    )
```

```python
import jax
import jax.numpy as jnp
from jax import lax
from jax.experimental import pallas as pl
from jax.experimental.pallas import tpu as pltpu
from jax.sharding import PartitionSpec as P

FF_WIN = 16384
MATS = 2
ROWS = 256
FIELDS = 2048
WIDE = 2304
RANK = 256
NZ, NX, NY = 8, 4, 4
KEEP = 0.95
EPS = 1e-06
F32 = jnp.float32
BF16 = jnp.bfloat16
VMEM = pl.BlockSpec(memory_space=pltpu.VMEM)
SMEM = pl.BlockSpec(memory_space=pltpu.SMEM)
PARAMS = pltpu.CompilerParams(vmem_limit_bytes=56 * 1024 * 1024)


def sds(*shape):
    return jax.ShapeDtypeStruct(shape, F32)


def call(body, ins, outs, scratch=(), flops=0, nbytes=0):
    return pl.pallas_call(
        body,
        out_shape=outs,
        in_specs=[SMEM] + [VMEM] * (len(ins) - 1),
        out_specs=[VMEM] * len(outs),
        scratch_shapes=list(scratch),
        compiler_params=PARAMS,
        cost_estimate=pl.CostEstimate(flops=flops, bytes_accessed=nbytes, transcendentals=0),
    )(*ins)


def send_row(value, dz, dx):
    pairs = [
        (z * NX + x, (z + dz) % NZ * NX + (x + dx) % NX) for z in range(NZ) for x in range(NX)
    ]
    return lax.ppermute(value, "row", pairs)


def send_z(value, step):
    return send_row(value, step, 0)


def send_x(value, step):
    return send_row(value, 0, step)


def send_y(value, step):
    pairs = [(y * 2 + c, (y + step) % NY * 2 + c) for y in range(NY) for c in range(2)]
    return lax.ppermute(value, "col", pairs)


def send_core(value):
    return lax.ppermute(value, "col", [(k, k ^ 1) for k in range(2 * NY)])


def ring_gather_whole(value, size, send):
    got = {0: value}
    ahead = behind = value
    for k in range(1, size // 2 + 1):
        ahead = send(ahead, 1)
        got[size - k] = ahead
        if k < size // 2:
            behind = send(behind, -1)
            got[k] = behind
    return [got[k] for k in range(size)]


def ring_scatter_whole(blocks, size, send):
    half = size // 2
    ahead, behind = send(blocks[half], 1), None
    for k in range(half - 1, 0, -1):
        ahead = send(ahead + blocks[k], 1)
        part = blocks[size - k]
        behind = send(part if behind is None else behind + part, -1)
    return blocks[0] + ahead + behind


def ring_gather(value, size, send):
    half = size // 2
    got = {0: value}
    ahead = behind = value
    for k in range(1, half):
        ahead, behind = send(ahead, 1), send(behind, -1)
        got[size - k] = ahead
        got[k] = behind
    cut = value.shape[0] // 2
    got[half] = (send(ahead[:cut], 1), send(behind[cut:], -1))
    return [got[k] for k in range(size)]


def exchange(blocks, axis, groups=None):
    return lax.all_to_all(blocks, axis, 0, 0, axis_index_groups=groups, tiled=True)


def spread(value, size, axis, groups=None):
    return exchange(jnp.broadcast_to(value[None], (size,) + value.shape), axis, groups)


Z_GROUPS = [[z * NX + x for z in range(NZ)] for x in range(NX)]


def ring_scatter(blocks, size, send):
    half = size // 2
    top, bottom = blocks[half]
    cut = top.shape[0]
    top, bottom = send(top, 1), send(bottom, -1)
    ahead, behind = blocks[half - 1], blocks[size - half + 1]
    ahead = jnp.concatenate([ahead[:cut] + top, ahead[cut:]], axis=0)
    behind = jnp.concatenate([behind[:cut], behind[cut:] + bottom], axis=0)
    for k in range(half - 1, 0, -1):
        ahead, behind = send(ahead, 1), send(behind, -1)
        if k > 1:
            ahead = ahead + blocks[k - 1]
            behind = behind + blocks[size - k + 1]
    return blocks[0] + ahead + behind


def gather_z(value):
    return lax.all_gather(value, "row", axis=0, tiled=True, axis_index_groups=Z_GROUPS)


def split(value):
    high = value.astype(BF16)
    return high, (value - high.astype(F32)).astype(BF16)


def dot(a, b):
    return jnp.dot(a, b, preferred_element_type=F32)


def dot3(a, b):
    return dot(a[0], b[0]) + (dot(a[0], b[1]) + dot(a[1], b[0]))


def dot_full(a, b):
    return jnp.dot(a, b, preferred_element_type=F32, precision=lax.Precision.HIGHEST)


def ring_at(at, k, size):
    return lax.rem(at + k, size)


def dsm(start, size, unit):
    return pl.ds(pl.multiple_of(start, unit), size)


def order_kernel(pos_ref, *refs):
    pieces, out_ref = refs[:NX], refs[NX]
    n = pieces[0].shape[0]
    for k in range(NX):
        out_ref[dsm(ring_at(pos_ref[1], k, NX) * n, n, n), :] = pieces[k][...]


def gather_x(pos, value):
    n, width = value.shape
    pieces = [value] + [send_x(value, -k) for k in range(1, NX)]
    return call(order_kernel, [pos] + pieces, [sds(NX * n, width)], nbytes=8 * n * width)[0]


def product_kernel(pos_ref, grad_ref, mom_ref, *refs):
    q0, q1, mine, other, q_scr, p_scr = refs[:8], refs[8:13], *refs[13:]
    z, x, y, c = (pos_ref[k] for k in range(4))
    for k in range(NZ):
        q_scr[0, dsm(ring_at(z, k, NZ) * 256, 256, 256), :] = q0[k][...]
    for k in range(NX):
        base = ring_at(x, k, NX) * 64
        for kz in range(NZ):
            if k == 2:
                block = q1[2 + kz // 4][pl.ds(kz % 4 * 64, 64), :]
            else:
                block = q1[k if k < 2 else 4][pl.ds(kz * 64, 64), :]
            q_scr[1, dsm(kz * 256 + base, 64, 64), :] = block
    for m in range(MATS):
        total = None
        for f in range(0, FIELDS, 512):
            b = mom_ref[m, :, f : f + 512] + grad_ref[m, :, f : f + 512].astype(F32)
            part = dot3(split(b), split(q_scr[m, f : f + 512, :]))
            total = part if total is None else total + part
        p_scr[m] = total
    for k in range(NY):
        at = ring_at(y, k, NY) * 32
        mine[k] = p_scr[:, dsm(c * 128 + at, 32, 32), :]
        other[k] = p_scr[:, dsm(128 - c * 128 + at, 32, 32), :]


def transposed_kernel(pos_ref, mine, other, grad_ref, mom_ref, p_ref, *refs):
    t0, t1, a_scr, b_scr = refs[:8], refs[8:13], *refs[13:]
    z, x = pos_ref[0], pos_ref[1]
    y, c = pos_ref[2], pos_ref[3]
    for k in range(NY):
        at = ring_at(y, k, NY) * 32
        p_ref[:, dsm(c * 128 + at, 32, 32), :] = mine[k]
        p_ref[:, dsm(128 - c * 128 + at, 32, 32), :] = other[k]
    for m in range(MATS):
        a_scr[...] = p_ref[m].T
        for kz in range(NZ):
            for kx in range(NX):
                zz, xx = ring_at(z, kz, NZ), ring_at(x, kx, NX)
                if m == 0:
                    to, at = (kz * NX + kx) * 8, (zz * NX + xx) * 8
                else:
                    to, at = (kx * NZ + kz) * 8, (xx * NZ + kz) * 8
                b_scr[m, to : to + 8, :] = a_scr[dsm(at, 8, 8), :]
        lhs = split(b_scr[m])
        for f in list(range(0, FIELDS, 512)) + [FIELDS]:
            if f < FIELDS:
                b = mom_ref[m, :, f : f + 512] + grad_ref[m, :, f : f + 512].astype(F32)
                out = dot3(lhs, split(b))
            else:
                out = dot_full(b_scr[m], p_ref[m])
            sizes = [32] * 8 if m == 0 else [64, 64, 32, 32, 64]
            at = 0
            for ref, size in zip(t0 if m == 0 else t1, sizes):
                ref[:, f : f + out.shape[1]] = out[at : at + size]
                at += size


BLOCK = 64


def invert_blocks(pair):
    shape = (8, 2 * BLOCK)
    lane = lax.broadcasted_iota(jnp.int32, shape, 1)
    sub = lax.broadcasted_iota(jnp.int32, shape, 0)
    first = lane < BLOCK
    at = lane % BLOCK

    def lanes(group, j):
        left = jnp.broadcast_to(group[:, j : j + 1], shape)
        return jnp.where(first, left, jnp.broadcast_to(group[:, BLOCK + j : BLOCK + j + 1], shape))

    groups = [pair[g : g + 8, :] for g in range(0, BLOCK, 8)]
    done = []
    for g in range(BLOCK // 8):
        scale = jnp.ones(shape, F32)
        for i in range(0, 8, 2):
            j = g * 8 + i
            here = groups[g]
            x, y = lanes(here, j), lanes(here, j + 1)
            a = jnp.broadcast_to(x[i : i + 1], shape)
            b = jnp.broadcast_to(x[i + 1 : i + 2], shape)
            c = jnp.broadcast_to(y[i + 1 : i + 2], shape)
            over_a = 1.0 / a
            det = a * c - b * b
            over_det = 1.0 / det
            row_j = jnp.broadcast_to(here[i : i + 1], shape)
            row_k = jnp.broadcast_to(here[i + 1 : i + 2], shape)
            in_j, in_k = at == j, at == j + 1
            pivots = in_j | in_k
            row_j = jnp.where(in_j, 1.0, jnp.where(in_k, 0.0, row_j))
            row_k = jnp.where(in_k, 1.0, jnp.where(in_j, 0.0, row_k)) - (b * over_a) * row_j
            for h in range(g, BLOCK // 8):
                if h > g:
                    x, y = lanes(groups[h], j), lanes(groups[h], j + 1)
                u = x * over_a
                v = (a * y - b * x) * over_det
                new = jnp.where(pivots, 0.0, groups[h]) - u * row_j - v * row_k
                if h == g:
                    new = jnp.where(sub > i + 1, new, here)
                    new = jnp.where(sub == i, row_j, jnp.where(sub == i + 1, row_k, new))
                groups[h] = new
            scale = jnp.where(sub == i, lax.rsqrt(a), scale)
            scale = jnp.where(sub == i + 1, lax.rsqrt(det * over_a), scale)
        done.append(jnp.where(sub + g * 8 >= at, groups[g] * scale, 0.0))
    packed = jnp.concatenate(done, axis=0)
    return [packed[:, :BLOCK], packed[:, BLOCK:]]


def cholesky_kernel(pos_ref, p_ref, *refs):
    gram, left_ref, x_ref, inv_ref, scr = refs
    rows = lax.broadcasted_iota(jnp.int32, (RANK, RANK), 0)
    cols = lax.broadcasted_iota(jnp.int32, (RANK, RANK), 1)
    for z in range(NZ):
        for x in range(NX):
            k = z * NX + x
            scr[0, k * 8 : k * 8 + 8, :] = gram[k, 0]
            scr[1, (x * NZ + z) * 8 : (x * NZ + z) * 8 + 8, :] = gram[k, 1]
    for m in range(MATS):
        scr[m] = scr[m] + jnp.where(rows == cols, EPS, 0.0)
    wide = lax.broadcasted_iota(jnp.int32, (BLOCK, RANK), 1)
    low = lax.broadcasted_iota(jnp.int32, (BLOCK, RANK), 0)
    for s in range(0, RANK, BLOCK):
        e = s + BLOCK
        inverse = invert_blocks(jnp.concatenate([scr[m, s:e, s:e] for m in range(MATS)], axis=1))
        for m in range(MATS):
            panel = scr[m, s : s + BLOCK, :]
            inside = (wide >= s) & (wide < s + BLOCK)
            panel = jnp.where(inside, jnp.where(wide == low + s, 1.0, 0.0), panel)
            panel = dot_full(inverse[m], panel)
            scr[m, s : s + BLOCK, :] = panel
            if e < RANK:
                low_edge = e // 128 * 128
                change = dot_full(panel[:, low_edge:].T, panel)
                below = jnp.where((cols[e:] >= s) & (cols[e:] < e), 0.0, scr[m, e:, :])
                scr[m, e:, :] = below - change[e - low_edge :]
    for m in range(MATS):
        inverse = jnp.where(rows >= cols, scr[m], 0.0)
        inv_ref[m] = inverse
        left = dot3(split(p_ref[m]), split(inverse.T))
        left_ref[m] = left
        x_ref[m] = (1.0 - KEEP) * dot3(split(left), split(inverse))


def assemble(pos_ref, t0, t1, scr):
    x = pos_ref[1]
    scr[0] = t0[...]
    for kx in range(NX):
        start = ring_at(x, kx, NX) * 64
        if kx == 2:
            scr[1, dsm(start, 32, 32), :] = t1[2][...]
            scr[1, dsm(start + 32, 32, 32), :] = t1[3][...]
        else:
            scr[1, dsm(start, 64, 64), :] = t1[kx if kx < 2 else 4][...]


def right_kernel(pos_ref, inv_ref, *refs):
    t0, t1, share_ref, sq_ref, scr, flip = refs[0], refs[1:6], refs[6], refs[7], refs[8], refs[9]
    assemble(pos_ref, t0, t1, scr)
    first = pos_ref[0] * 256 + pos_ref[1] * 64
    start = first // 128 * 128
    for m in range(MATS):
        lhs = split(inv_ref[m])
        total = jnp.zeros((RANK, 128), F32)
        for f in range(0, FIELDS, 512):
            out = dot3(lhs, split(scr[m, :, f : f + 512]))
            sq = out * out
            total += (sq[:, :128] + sq[:, 128:256]) + (sq[:, 256:384] + sq[:, 384:])
        sq_ref[m : m + 1, :] = jnp.sum(total.T, axis=0, keepdims=True)
        flip[...] = dot3(lhs, split(scr[m, :, dsm(start, 128, 128)])).T
        share_ref[m] = flip[dsm(first - start, 64, 64), :]


def feedback_kernel(pos_ref, x_ref, grad_ref, mom_ref, *refs):
    t0, t1, out_ref, scr = refs[0], refs[1:6], refs[6], refs[7]
    assemble(pos_ref, t0, t1, scr)
    for m in range(MATS):
        lhs = split(x_ref[m])
        for f in range(0, FIELDS, 512):
            out = dot3(lhs, split(scr[m, :, f : f + 512]))
            b = mom_ref[m, :, f : f + 512] + grad_ref[m, :, f : f + 512].astype(F32)
            out_ref[m, :, f : f + 512] = b - out


def flatten(parts):
    flat = []
    for part in parts:
        flat.extend(part if isinstance(part, tuple) else [part])
    return flat


def pair(parts, half):
    return parts[:half] + [(parts[half], parts[half + 1])] + parts[half + 2 :]


def per_device(gradient, momentum, prior_input_frame):
    row, col = lax.axis_index("row"), lax.axis_index("col")
    x_at = row % NX
    pos = jnp.stack([row // NX, x_at, col // 2, col % 2]).astype(jnp.int32)
    q = prior_input_frame[:, 0]

    q1 = gather_z(q[1])
    q0 = ring_gather_whole(gather_x(pos, q[0]), NZ, send_z)
    q1 = flatten(ring_gather(q1, NX, send_x))

    mine, other = call(
        product_kernel,
        [pos, gradient, momentum] + q0 + q1,
        [sds(NY, MATS, 32, RANK)] * 2,
        [pltpu.VMEM((MATS, FIELDS, RANK), F32), pltpu.VMEM((MATS, ROWS, RANK), F32)],
        flops=6 * MATS * ROWS * FIELDS * RANK,
        nbytes=11 << 20,
    )
    other = send_core(other)
    mine = [mine[k] + other[k] for k in range(NY)]
    share = mine[0] + sum(send_y(mine[k], k) for k in range(1, NY))
    mine = jnp.stack([share] + [send_y(share, -k) for k in range(1, NY)])
    other = send_core(mine)
    sizes0, sizes1 = [32] * 8, [64, 64, 32, 32, 64]
    product, *parts = call(
        transposed_kernel,
        [pos, mine, other, gradient, momentum],
        [sds(MATS, ROWS, RANK)] + [sds(n, WIDE) for n in sizes0 + sizes1],
        [pltpu.VMEM((RANK, ROWS), F32), pltpu.VMEM((MATS, RANK, ROWS), F32)],
        flops=6 * MATS * ROWS * FIELDS * RANK,
        nbytes=11 << 20,
    )
    share0 = ring_scatter_whole(list(parts[:8]), NZ, send_z)
    share1 = ring_scatter(pair(list(parts[8:]), 2), NX, send_x)
    pieces = [share0[k * 8 : k * 8 + 8] for k in range(NX)]
    share0 = pieces[0] + sum(send_x(pieces[k], k) for k in range(1, NX))
    share1 = jnp.sum(exchange(share1.reshape(NZ, 8, WIDE), "row", Z_GROUPS), axis=0)
    t1 = flatten(ring_gather(gather_z(share1[:, :FIELDS]), NX, send_x))
    t0 = gather_z(gather_x(pos, share0[:, :FIELDS]))
    gram = spread(jnp.stack([share0[:, FIELDS:], share1[:, FIELDS:]]), 32, "row")

    left_basis, weights, inverse = call(
        cholesky_kernel,
        [pos, product, gram],
        [sds(MATS, ROWS, RANK)] * 3,
        [pltpu.VMEM((MATS, RANK, RANK), F32)],
        flops=1 << 34,
        nbytes=2 << 20,
    )
    tall = pltpu.VMEM((MATS, RANK, FIELDS), F32)
    share, squares = call(
        right_kernel,
        [pos, inverse, t0] + t1,
        [sds(MATS, 64, RANK), sds(MATS, RANK)],
        [tall, pltpu.VMEM((128, RANK), F32)],
        flops=6 * MATS * ROWS * FIELDS * RANK,
        nbytes=5 << 20,
    )
    total = jnp.sum(spread(squares, 8, "col"), axis=0)
    (momentum_next,) = call(
        feedback_kernel,
        [pos, weights, gradient, momentum, t0] + t1,
        [sds(MATS, ROWS, FIELDS)],
        [tall],
        flops=6 * MATS * ROWS * FIELDS * RANK,
        nbytes=15 << 20,
    )
    fresh = share * lax.rsqrt(total / FF_WIN + EPS)[:, None]
    return momentum_next, left_basis, fresh[:, None]


def solution(mesh):
    return jax.shard_map(
        per_device,
        mesh=mesh,
        in_specs=(P(None, "row", "col"), P(None, "row", "col"), P(None, "col", "row", None)),
        out_specs=(P(None, "row", "col"), P(None, "row", None), P(None, "col", "row", None)),
        check_vma=False,
    )
```

```python
import jax
import jax.numpy as jnp
from jax import lax
from jax.experimental import pallas as pl
from jax.experimental.pallas import tpu as pltpu
from jax.sharding import PartitionSpec as P

FF_WIN = 16384
MATS = 2
ROWS = 256
FIELDS = 2048
WIDE = 2304
RANK = 256
NZ, NX, NY = 8, 4, 4
KEEP = 0.95
EPS = 1e-06
F32 = jnp.float32
BF16 = jnp.bfloat16
VMEM = pl.BlockSpec(memory_space=pltpu.VMEM)
SMEM = pl.BlockSpec(memory_space=pltpu.SMEM)
PARAMS = pltpu.CompilerParams(vmem_limit_bytes=24 * 1024 * 1024)


def sds(*shape):
    return jax.ShapeDtypeStruct(shape, F32)


def call(body, ins, outs, scratch=(), flops=0, nbytes=0):
    return pl.pallas_call(
        body,
        out_shape=outs,
        in_specs=[SMEM] + [VMEM] * (len(ins) - 1),
        out_specs=[VMEM] * len(outs),
        scratch_shapes=list(scratch),
        compiler_params=PARAMS,
        cost_estimate=pl.CostEstimate(flops=flops, bytes_accessed=nbytes, transcendentals=0),
    )(*ins)


def send_row(value, dz, dx):
    pairs = [
        (z * NX + x, (z + dz) % NZ * NX + (x + dx) % NX) for z in range(NZ) for x in range(NX)
    ]
    return lax.ppermute(value, "row", pairs)


def send_z(value, step):
    return send_row(value, step, 0)


def send_x(value, step):
    return send_row(value, 0, step)


def send_y(value, step):
    pairs = [(y * 2 + c, (y + step) % NY * 2 + c) for y in range(NY) for c in range(2)]
    return lax.ppermute(value, "col", pairs)


def send_core(value):
    return lax.ppermute(value, "col", [(k, k ^ 1) for k in range(2 * NY)])


def ring_gather_whole(value, size, send):
    got = {0: value}
    ahead = behind = value
    for k in range(1, size // 2 + 1):
        ahead = send(ahead, 1)
        got[size - k] = ahead
        if k < size // 2:
            behind = send(behind, -1)
            got[k] = behind
    return [got[k] for k in range(size)]


def ring_scatter_whole(blocks, size, send):
    half = size // 2
    ahead, behind = send(blocks[half], 1), None
    for k in range(half - 1, 0, -1):
        ahead = send(ahead + blocks[k], 1)
        part = blocks[size - k]
        behind = send(part if behind is None else behind + part, -1)
    return blocks[0] + ahead + behind


def ring_gather(value, size, send):
    half = size // 2
    got = {0: value}
    ahead = behind = value
    for k in range(1, half):
        ahead, behind = send(ahead, 1), send(behind, -1)
        got[size - k] = ahead
        got[k] = behind
    cut = value.shape[0] // 2
    got[half] = (send(ahead[:cut], 1), send(behind[cut:], -1))
    return [got[k] for k in range(size)]


def exchange(blocks, axis, groups=None):
    return lax.all_to_all(blocks, axis, 0, 0, axis_index_groups=groups, tiled=True)


def spread(value, size, axis, groups=None):
    return exchange(jnp.broadcast_to(value[None], (size,) + value.shape), axis, groups)


Z_GROUPS = [[z * NX + x for z in range(NZ)] for x in range(NX)]


def ring_scatter(blocks, size, send):
    half = size // 2
    top, bottom = blocks[half]
    cut = top.shape[0]
    top, bottom = send(top, 1), send(bottom, -1)
    ahead, behind = blocks[half - 1], blocks[size - half + 1]
    ahead = jnp.concatenate([ahead[:cut] + top, ahead[cut:]], axis=0)
    behind = jnp.concatenate([behind[:cut], behind[cut:] + bottom], axis=0)
    for k in range(half - 1, 0, -1):
        ahead, behind = send(ahead, 1), send(behind, -1)
        if k > 1:
            ahead = ahead + blocks[k - 1]
            behind = behind + blocks[size - k + 1]
    return blocks[0] + ahead + behind


def gather_z(value):
    return spread(value, NZ, "row", Z_GROUPS).reshape(NZ * value.shape[0], value.shape[1])


def split(value):
    high = value.astype(BF16)
    return high, (value - high.astype(F32)).astype(BF16)


def dot(a, b):
    return jnp.dot(a, b, preferred_element_type=F32)


def dot3(a, b):
    return dot(a[0], b[0]) + (dot(a[0], b[1]) + dot(a[1], b[0]))


def dot_full(a, b):
    return jnp.dot(a, b, preferred_element_type=F32, precision=lax.Precision.HIGHEST)


def ring_at(at, k, size):
    return lax.rem(at + k, size)


def dsm(start, size, unit):
    return pl.ds(pl.multiple_of(start, unit), size)


def order_kernel(pos_ref, *refs):
    pieces, out_ref = refs[:NX], refs[NX]
    n = pieces[0].shape[0]
    for k in range(NX):
        out_ref[dsm(ring_at(pos_ref[1], k, NX) * n, n, n), :] = pieces[k][...]


def gather_x(pos, value):
    n, width = value.shape
    pieces = [value] + [send_x(value, -k) for k in range(1, NX)]
    return call(order_kernel, [pos] + pieces, [sds(NX * n, width)], nbytes=8 * n * width)[0]


def product_kernel(pos_ref, grad_ref, mom_ref, *refs):
    q0, q1, mine, other, q_scr, p_scr = refs[:8], refs[8:13], *refs[13:]
    z, x, y, c = (pos_ref[k] for k in range(4))
    for k in range(NZ):
        q_scr[0, dsm(ring_at(z, k, NZ) * 256, 256, 256), :] = q0[k][...]
    for k in range(NX):
        base = ring_at(x, k, NX) * 64
        for kz in range(NZ):
            if k == 2:
                block = q1[2 + kz // 4][pl.ds(kz % 4 * 64, 64), :]
            else:
                block = q1[k if k < 2 else 4][pl.ds(kz * 64, 64), :]
            q_scr[1, dsm(kz * 256 + base, 64, 64), :] = block
    for m in range(MATS):
        total = None
        for f in range(0, FIELDS, 512):
            b = mom_ref[m, :, f : f + 512] + grad_ref[m, :, f : f + 512].astype(F32)
            part = dot3(split(b), split(q_scr[m, f : f + 512, :]))
            total = part if total is None else total + part
        p_scr[m] = total
    for k in range(NY):
        at = ring_at(y, k, NY) * 32
        mine[k] = p_scr[:, dsm(c * 128 + at, 32, 32), :]
        other[k] = p_scr[:, dsm(128 - c * 128 + at, 32, 32), :]


def transposed_kernel(pos_ref, mine, other, grad_ref, mom_ref, p_ref, *refs):
    t0, t1, a_scr, b_scr = refs[:8], refs[8:13], *refs[13:]
    z, x = pos_ref[0], pos_ref[1]
    y, c = pos_ref[2], pos_ref[3]
    for k in range(NY):
        at = ring_at(y, k, NY) * 32
        p_ref[:, dsm(c * 128 + at, 32, 32), :] = mine[k]
        p_ref[:, dsm(128 - c * 128 + at, 32, 32), :] = other[k]
    for m in range(MATS):
        a_scr[...] = p_ref[m].T
        for kz in range(NZ):
            for kx in range(NX):
                zz, xx = ring_at(z, kz, NZ), ring_at(x, kx, NX)
                if m == 0:
                    to, at = (kz * NX + kx) * 8, (zz * NX + xx) * 8
                else:
                    to, at = (kx * NZ + kz) * 8, (xx * NZ + kz) * 8
                b_scr[m, to : to + 8, :] = a_scr[dsm(at, 8, 8), :]
        lhs = split(b_scr[m])
        for f in list(range(0, FIELDS, 512)) + [FIELDS]:
            if f < FIELDS:
                b = mom_ref[m, :, f : f + 512] + grad_ref[m, :, f : f + 512].astype(F32)
                out = dot3(lhs, split(b))
            else:
                out = dot_full(b_scr[m], p_ref[m])
            sizes = [32] * 8 if m == 0 else [64, 64, 32, 32, 64]
            at = 0
            for ref, size in zip(t0 if m == 0 else t1, sizes):
                ref[:, f : f + out.shape[1]] = out[at : at + size]
                at += size


BLOCK = 64


def invert_blocks(pair):
    shape = (8, 2 * BLOCK)
    lane = lax.broadcasted_iota(jnp.int32, shape, 1)
    sub = lax.broadcasted_iota(jnp.int32, shape, 0)
    first = lane < BLOCK
    at = lane % BLOCK

    def lanes(group, j):
        left = jnp.broadcast_to(group[:, j : j + 1], shape)
        return jnp.where(first, left, jnp.broadcast_to(group[:, BLOCK + j : BLOCK + j + 1], shape))

    groups = [pair[g : g + 8, :] for g in range(0, BLOCK, 8)]
    done = []
    for g in range(BLOCK // 8):
        scale = jnp.ones(shape, F32)
        for i in range(0, 8, 2):
            j = g * 8 + i
            here = groups[g]
            x, y = lanes(here, j), lanes(here, j + 1)
            a = jnp.broadcast_to(x[i : i + 1], shape)
            b = jnp.broadcast_to(x[i + 1 : i + 2], shape)
            c = jnp.broadcast_to(y[i + 1 : i + 2], shape)
            over_a = 1.0 / a
            det = a * c - b * b
            over_det = 1.0 / det
            row_j = jnp.broadcast_to(here[i : i + 1], shape)
            row_k = jnp.broadcast_to(here[i + 1 : i + 2], shape)
            in_j, in_k = at == j, at == j + 1
            pivots = in_j | in_k
            row_j = jnp.where(in_j, 1.0, jnp.where(in_k, 0.0, row_j))
            row_k = jnp.where(in_k, 1.0, jnp.where(in_j, 0.0, row_k)) - (b * over_a) * row_j
            for h in range(g, BLOCK // 8):
                if h > g:
                    x, y = lanes(groups[h], j), lanes(groups[h], j + 1)
                u = x * over_a
                v = (a * y - b * x) * over_det
                new = jnp.where(pivots, 0.0, groups[h]) - u * row_j - v * row_k
                if h == g:
                    new = jnp.where(sub > i + 1, new, here)
                    new = jnp.where(sub == i, row_j, jnp.where(sub == i + 1, row_k, new))
                groups[h] = new
            scale = jnp.where(sub == i, lax.rsqrt(a), scale)
            scale = jnp.where(sub == i + 1, lax.rsqrt(det * over_a), scale)
        done.append(jnp.where(sub + g * 8 >= at, groups[g] * scale, 0.0))
    packed = jnp.concatenate(done, axis=0)
    return [packed[:, :BLOCK], packed[:, BLOCK:]]


def turn(value, start):
    return pltpu.roll(value, lax.rem(RANK - start, RANK), 1)


def cholesky_kernel(pos_ref, p_ref, *refs):
    gram, left_ref, x_ref, inv_ref, scr = refs
    rows = lax.broadcasted_iota(jnp.int32, (RANK, RANK), 0)
    cols = lax.broadcasted_iota(jnp.int32, (RANK, RANK), 1)
    for z in range(NZ):
        for x in range(NX):
            k = z * NX + x
            scr[0, k * 8 : k * 8 + 8, :] = gram[k, 0]
            scr[1, (x * NZ + z) * 8 : (x * NZ + z) * 8 + 8, :] = gram[k, 1]
    for m in range(MATS):
        scr[m] = scr[m] + jnp.where(rows == cols, EPS, 0.0)
    wide = lax.broadcasted_iota(jnp.int32, (BLOCK, RANK), 1)
    low = lax.broadcasted_iota(jnp.int32, (BLOCK, RANK), 0)
    for s in range(0, RANK, BLOCK):
        e = s + BLOCK
        inverse = invert_blocks(jnp.concatenate([scr[m, s:e, s:e] for m in range(MATS)], axis=1))
        for m in range(MATS):
            panel = scr[m, s : s + BLOCK, :]
            inside = (wide >= s) & (wide < s + BLOCK)
            panel = jnp.where(inside, jnp.where(wide == low + s, 1.0, 0.0), panel)
            panel = dot_full(inverse[m], panel)
            scr[m, s : s + BLOCK, :] = panel
            if e < RANK:
                low_edge = e // 128 * 128
                change = dot_full(panel[:, low_edge:].T, panel)
                below = jnp.where((cols[e:] >= s) & (cols[e:] < e), 0.0, scr[m, e:, :])
                scr[m, e:, :] = below - change[e - low_edge :]
    for m in range(MATS):
        inverse = jnp.where(rows >= cols, scr[m], 0.0)
        start = pos_ref[m] * (64 if m else 32)
        inv_ref[m] = turn(inverse, start)
        left = dot3(split(p_ref[m]), split(inverse.T))
        left_ref[m] = left
        x_ref[m] = turn((1.0 - KEEP) * dot3(split(left), split(inverse)), start)


CHUNK = 512
T_ROWS = [32] * NZ, [64, 64, 32, 32, 64]


def t_specs(index):
    return [pl.BlockSpec((n, CHUNK), index[m]) for m in range(MATS) for n in T_ROWS[m]]


def stacked(refs):
    return split(jnp.concatenate([ref[...] for ref in refs], axis=0))


def right_kernel(pos_ref, inv_ref, *refs):
    t0, t1, share_ref, sq_ref, out_scr, total, flip = refs[:8], refs[8:13], *refs[13:]
    m, f = pl.program_id(0), pl.program_id(1)
    lhs = split(inv_ref[0])

    @pl.when(m == 0)
    def _():
        out_scr[...] = dot3(lhs, stacked(t0))

    @pl.when(m == 1)
    def _():
        out_scr[...] = dot3(lhs, stacked(t1))

    @pl.when(f == 0)
    def _():
        total[...] = jnp.zeros_like(total)

    sq = out_scr[...] * out_scr[...]
    total[...] += (sq[:, :128] + sq[:, 128:256]) + (sq[:, 256:384] + sq[:, 384:])

    @pl.when(f == FIELDS // CHUNK - 1)
    def _():
        sq_ref[0] = jnp.sum(total[...].T, axis=0, keepdims=True)

    first = pos_ref[0] * 256 + pos_ref[1] * 64

    @pl.when(f == first // CHUNK)
    def _():
        local = lax.rem(first, CHUNK)
        start = local // 128 * 128
        flip[...] = out_scr[:, dsm(start, 128, 128)].T
        share_ref[0] = flip[dsm(local - start, 64, 64), :]


def right_factor(pos, inverse, t):
    index = (
        lambda m, f: (0, jnp.where(m == 0, f, FIELDS // CHUNK - 1)),
        lambda m, f: (0, jnp.where(m == 0, 0, f)),
    )
    return pl.pallas_call(
        right_kernel,
        grid=(MATS, FIELDS // CHUNK),
        out_shape=[sds(MATS, 64, RANK), sds(MATS, 1, RANK)],
        in_specs=[SMEM, pl.BlockSpec((1, RANK, RANK), lambda m, f: (m, 0, 0))] + t_specs(index),
        out_specs=[
            pl.BlockSpec((1, 64, RANK), lambda m, f: (m, 0, 0)),
            pl.BlockSpec((1, 1, RANK), lambda m, f: (m, 0, 0)),
        ],
        scratch_shapes=[
            pltpu.VMEM((RANK, CHUNK), F32),
            pltpu.VMEM((RANK, 128), F32),
            pltpu.VMEM((128, RANK), F32),
        ],
        compiler_params=PARAMS,
        cost_estimate=pl.CostEstimate(flops=1 << 32, bytes_accessed=5 << 20, transcendentals=0),
    )(pos, inverse, *t)


def feedback_kernel(x_ref, grad_ref, mom_ref, *refs):
    t, out_ref = refs[:-1], refs[-1]
    out = dot3(split(x_ref[0]), stacked(t))
    out_ref[0] = mom_ref[0] + grad_ref[0].astype(F32) - out


def feedback_second(x_ref, grad_ref, mom_ref, *refs):
    feedback_kernel(x_ref, grad_ref, mom_ref, *refs[:-2], refs[-1])


def feedback(m, weights, gradient, momentum, t, before=()):
    block = pl.BlockSpec((1, ROWS, CHUNK), lambda f: (m, 0, f))
    return pl.pallas_call(
        feedback_second if before else feedback_kernel,
        grid=(FIELDS // CHUNK,),
        out_shape=sds(MATS, ROWS, FIELDS),
        in_specs=[pl.BlockSpec((1, RANK, RANK), lambda f: (m, 0, 0)), block, block]
        + [pl.BlockSpec((n, CHUNK), lambda f: (0, f)) for n in T_ROWS[m]]
        + [pl.BlockSpec(memory_space=pl.ANY)] * len(before),
        out_specs=block,
        input_output_aliases={3 + len(t): 0} if before else {},
        compiler_params=PARAMS,
        cost_estimate=pl.CostEstimate(flops=1 << 31, bytes_accessed=7 << 20, transcendentals=0),
    )(weights, gradient, momentum, *t, *before)


def flatten(parts):
    flat = []
    for part in parts:
        flat.extend(part if isinstance(part, tuple) else [part])
    return flat


def pair(parts, half):
    return parts[:half] + [(parts[half], parts[half + 1])] + parts[half + 2 :]


def per_device(gradient, momentum, prior_input_frame):
    row, col = lax.axis_index("row"), lax.axis_index("col")
    x_at = row % NX
    pos = jnp.stack([row // NX, x_at, col // 2, col % 2]).astype(jnp.int32)
    q = prior_input_frame[:, 0]

    q1 = gather_z(q[1])
    q0 = ring_gather_whole(gather_x(pos, q[0]), NZ, send_z)
    q1 = flatten(ring_gather(q1, NX, send_x))

    mine, other = call(
        product_kernel,
        [pos, gradient, momentum] + q0 + q1,
        [sds(NY, MATS, 32, RANK)] * 2,
        [pltpu.VMEM((MATS, FIELDS, RANK), F32), pltpu.VMEM((MATS, ROWS, RANK), F32)],
        flops=6 * MATS * ROWS * FIELDS * RANK,
        nbytes=11 << 20,
    )
    other = send_core(other)
    mine = [mine[k] + other[k] for k in range(NY)]
    share = mine[0] + sum(send_y(mine[k], k) for k in range(1, NY))
    mine = jnp.stack([share] + [send_y(share, -k) for k in range(1, NY)])
    other = send_core(mine)
    sizes0, sizes1 = [32] * 8, [64, 64, 32, 32, 64]
    product, *parts = call(
        transposed_kernel,
        [pos, mine, other, gradient, momentum],
        [sds(MATS, ROWS, RANK)] + [sds(n, WIDE) for n in sizes0 + sizes1],
        [pltpu.VMEM((RANK, ROWS), F32), pltpu.VMEM((MATS, RANK, ROWS), F32)],
        flops=6 * MATS * ROWS * FIELDS * RANK,
        nbytes=11 << 20,
    )
    share0 = ring_scatter_whole(list(parts[:8]), NZ, send_z)
    share1 = ring_scatter(pair(list(parts[8:]), 2), NX, send_x)
    pieces = [share0[k * 8 : k * 8 + 8] for k in range(NX)]
    share0 = pieces[0] + sum(send_x(pieces[k], k) for k in range(1, NX))
    share1 = jnp.sum(exchange(share1.reshape(NZ, 8, WIDE), "row", Z_GROUPS), axis=0)
    t1 = flatten(ring_gather(gather_z(share1[:, :FIELDS]), NX, send_x))
    t0 = ring_gather_whole(gather_x(pos, share0[:, :FIELDS]), NZ, send_z)
    gram = spread(jnp.stack([share0[:, FIELDS:], share1[:, FIELDS:]]), 32, "row")

    left_basis, weights, inverse = call(
        cholesky_kernel,
        [pos, product, gram],
        [sds(MATS, ROWS, RANK)] * 3,
        [pltpu.VMEM((MATS, RANK, RANK), F32)],
        flops=1 << 34,
        nbytes=2 << 20,
    )
    share, squares = right_factor(pos, inverse, t0 + t1)
    squares = squares[:, 0]
    momentum_next = feedback(0, weights, gradient, momentum, t0)
    total = squares + sum(send_y(squares, k) for k in range(1, NY))
    total = total + send_core(total)
    momentum_next = feedback(1, weights, gradient, momentum, t1, (momentum_next,))
    fresh = share * lax.rsqrt(total / FF_WIN + EPS)[:, None]
    return momentum_next, left_basis, fresh[:, None]


def solution(mesh):
    return jax.shard_map(
        per_device,
        mesh=mesh,
        in_specs=(P(None, "row", "col"), P(None, "row", "col"), P(None, "col", "row", None)),
        out_specs=(P(None, "row", "col"), P(None, "row", None), P(None, "col", "row", None)),
        check_vma=False,
    )
```

```python
import jax
import jax.numpy as jnp
from jax import lax
from jax.experimental import pallas as pl
from jax.experimental.pallas import tpu as pltpu
from jax.sharding import PartitionSpec as P

FF_WIN = 16384
MATS = 2
ROWS = 256
FIELDS = 2048
WIDE = 2304
RANK = 256
NZ, NX, NY = 8, 4, 4
KEEP = 0.95
EPS = 1e-06
F32 = jnp.float32
BF16 = jnp.bfloat16
VMEM = pl.BlockSpec(memory_space=pltpu.VMEM)
SMEM = pl.BlockSpec(memory_space=pltpu.SMEM)
PARAMS = pltpu.CompilerParams(vmem_limit_bytes=24 * 1024 * 1024)


def sds(*shape):
    return jax.ShapeDtypeStruct(shape, F32)


def call(body, ins, outs, scratch=(), flops=0, nbytes=0):
    return pl.pallas_call(
        body,
        out_shape=outs,
        in_specs=[SMEM] + [VMEM] * (len(ins) - 1),
        out_specs=[VMEM] * len(outs),
        scratch_shapes=list(scratch),
        compiler_params=PARAMS,
        cost_estimate=pl.CostEstimate(flops=flops, bytes_accessed=nbytes, transcendentals=0),
    )(*ins)


def send_row(value, dz, dx):
    pairs = [
        (z * NX + x, (z + dz) % NZ * NX + (x + dx) % NX) for z in range(NZ) for x in range(NX)
    ]
    return lax.ppermute(value, "row", pairs)


def send_z(value, step):
    return send_row(value, step, 0)


def send_x(value, step):
    return send_row(value, 0, step)


def send_y(value, step):
    pairs = [(y * 2 + c, (y + step) % NY * 2 + c) for y in range(NY) for c in range(2)]
    return lax.ppermute(value, "col", pairs)


def send_core(value):
    return lax.ppermute(value, "col", [(k, k ^ 1) for k in range(2 * NY)])


def ring_gather_whole(value, size, send):
    got = {0: value}
    ahead = behind = value
    for k in range(1, size // 2 + 1):
        ahead = send(ahead, 1)
        got[size - k] = ahead
        if k < size // 2:
            behind = send(behind, -1)
            got[k] = behind
    return [got[k] for k in range(size)]


def ring_scatter_whole(blocks, size, send):
    half = size // 2
    ahead, behind = send(blocks[half], 1), None
    for k in range(half - 1, 0, -1):
        ahead = send(ahead + blocks[k], 1)
        part = blocks[size - k]
        behind = send(part if behind is None else behind + part, -1)
    return blocks[0] + ahead + behind


def ring_gather(value, size, send):
    half = size // 2
    got = {0: value}
    ahead = behind = value
    for k in range(1, half):
        ahead, behind = send(ahead, 1), send(behind, -1)
        got[size - k] = ahead
        got[k] = behind
    cut = value.shape[0] // 2
    got[half] = (send(ahead[:cut], 1), send(behind[cut:], -1))
    return [got[k] for k in range(size)]


def exchange(blocks, axis, groups=None):
    return lax.all_to_all(blocks, axis, 0, 0, axis_index_groups=groups, tiled=True)


def spread(value, size, axis, groups=None):
    return exchange(jnp.broadcast_to(value[None], (size,) + value.shape), axis, groups)


Z_GROUPS = [[z * NX + x for z in range(NZ)] for x in range(NX)]


def ring_scatter(blocks, size, send):
    half = size // 2
    top, bottom = blocks[half]
    cut = top.shape[0]
    top, bottom = send(top, 1), send(bottom, -1)
    ahead, behind = blocks[half - 1], blocks[size - half + 1]
    ahead = jnp.concatenate([ahead[:cut] + top, ahead[cut:]], axis=0)
    behind = jnp.concatenate([behind[:cut], behind[cut:] + bottom], axis=0)
    for k in range(half - 1, 0, -1):
        ahead, behind = send(ahead, 1), send(behind, -1)
        if k > 1:
            ahead = ahead + blocks[k - 1]
            behind = behind + blocks[size - k + 1]
    return blocks[0] + ahead + behind


def gather_z(value):
    return spread(value, NZ, "row", Z_GROUPS).reshape(NZ * value.shape[0], value.shape[1])


def split(value):
    high = value.astype(BF16)
    return high, (value - high.astype(F32)).astype(BF16)


def dot(a, b):
    return jnp.dot(a, b, preferred_element_type=F32)


def dot3(a, b):
    return dot(a[0], b[0]) + (dot(a[0], b[1]) + dot(a[1], b[0]))


def dot_full(a, b):
    return jnp.dot(a, b, preferred_element_type=F32, precision=lax.Precision.HIGHEST)


def ring_at(at, k, size):
    return lax.rem(at + k, size)


def dsm(start, size, unit):
    return pl.ds(pl.multiple_of(start, unit), size)


def order_kernel(pos_ref, *refs):
    pieces, out_ref = refs[:NX], refs[NX]
    n = pieces[0].shape[0]
    for k in range(NX):
        out_ref[dsm(ring_at(pos_ref[1], k, NX) * n, n, n), :] = pieces[k][...]


def order_and_copy_kernel(pos_ref, *refs):
    order_kernel(pos_ref, *refs[:NX], refs[NX + 1])
    for k in range(NZ):
        refs[NX + 2][k] = refs[NX][...]


def gather_x(pos, value, copied=None):
    n, width = value.shape
    pieces = [value] + [send_x(value, -k) for k in range(1, NX)]
    if copied is not None:
        return call(
            order_and_copy_kernel,
            [pos] + pieces + [copied],
            [sds(NX * n, width), sds(NZ, n, width)],
            nbytes=20 * n * width,
        )
    return call(order_kernel, [pos] + pieces, [sds(NX * n, width)], nbytes=8 * n * width)[0]


def product_kernel(pos_ref, grad_ref, mom_ref, *refs):
    q0, q1, mine, other, q_scr, p_scr = refs[:8], refs[8:13], *refs[13:]
    z, x, y, c = (pos_ref[k] for k in range(4))
    for k in range(NZ):
        q_scr[0, dsm(ring_at(z, k, NZ) * 256, 256, 256), :] = q0[k][...]
    for k in range(NX):
        base = ring_at(x, k, NX) * 64
        for kz in range(NZ):
            if k == 2:
                block = q1[2 + kz // 4][pl.ds(kz % 4 * 64, 64), :]
            else:
                block = q1[k if k < 2 else 4][pl.ds(kz * 64, 64), :]
            q_scr[1, dsm(kz * 256 + base, 64, 64), :] = block
    for m in range(MATS):
        total = None
        for f in range(0, FIELDS, 512):
            b = mom_ref[m, :, f : f + 512] + grad_ref[m, :, f : f + 512].astype(F32)
            part = dot3(split(b), split(q_scr[m, f : f + 512, :]))
            total = part if total is None else total + part
        p_scr[m] = total
    for k in range(NY):
        at = ring_at(y, k, NY) * 32
        mine[k] = p_scr[:, dsm(c * 128 + at, 32, 32), :]
        other[k] = p_scr[:, dsm(128 - c * 128 + at, 32, 32), :]


def transposed_kernel(pos_ref, mine, other, grad_ref, mom_ref, p_ref, *refs):
    t0, t1, a_scr, b_scr = refs[:8], refs[8:13], *refs[13:]
    z, x = pos_ref[0], pos_ref[1]
    y, c = pos_ref[2], pos_ref[3]
    for k in range(NY):
        at = ring_at(y, k, NY) * 32
        p_ref[:, dsm(c * 128 + at, 32, 32), :] = mine[k]
        p_ref[:, dsm(128 - c * 128 + at, 32, 32), :] = other[k]
    for m in range(MATS):
        a_scr[...] = p_ref[m].T
        for kz in range(NZ):
            for kx in range(NX):
                zz, xx = ring_at(z, kz, NZ), ring_at(x, kx, NX)
                if m == 0:
                    to, at = (kz * NX + kx) * 8, (zz * NX + xx) * 8
                else:
                    to, at = (kx * NZ + kz) * 8, (xx * NZ + kz) * 8
                b_scr[m, to : to + 8, :] = a_scr[dsm(at, 8, 8), :]
        lhs = split(b_scr[m])
        for f in list(range(0, FIELDS, 512)) + [FIELDS]:
            if f < FIELDS:
                b = mom_ref[m, :, f : f + 512] + grad_ref[m, :, f : f + 512].astype(F32)
                out = dot3(lhs, split(b))
            else:
                out = dot_full(b_scr[m], p_ref[m])
            sizes = [32] * 8 if m == 0 else [64, 64, 32, 32, 64]
            at = 0
            for ref, size in zip(t0 if m == 0 else t1, sizes):
                ref[:, f : f + out.shape[1]] = out[at : at + size]
                at += size


BLOCK = 64


def invert_blocks(pair):
    shape = (8, 2 * BLOCK)
    lane = lax.broadcasted_iota(jnp.int32, shape, 1)
    sub = lax.broadcasted_iota(jnp.int32, shape, 0)
    first = lane < BLOCK
    at = lane % BLOCK

    def lanes(group, j):
        left = jnp.broadcast_to(group[:, j : j + 1], shape)
        return jnp.where(first, left, jnp.broadcast_to(group[:, BLOCK + j : BLOCK + j + 1], shape))

    groups = [pair[g : g + 8, :] for g in range(0, BLOCK, 8)]
    done = []
    for g in range(BLOCK // 8):
        scale = jnp.ones(shape, F32)
        for i in range(0, 8, 2):
            j = g * 8 + i
            here = groups[g]
            x, y = lanes(here, j), lanes(here, j + 1)
            a = jnp.broadcast_to(x[i : i + 1], shape)
            b = jnp.broadcast_to(x[i + 1 : i + 2], shape)
            c = jnp.broadcast_to(y[i + 1 : i + 2], shape)
            over_a = 1.0 / a
            det = a * c - b * b
            over_det = 1.0 / det
            row_j = jnp.broadcast_to(here[i : i + 1], shape)
            row_k = jnp.broadcast_to(here[i + 1 : i + 2], shape)
            in_j, in_k = at == j, at == j + 1
            pivots = in_j | in_k
            row_j = jnp.where(in_j, 1.0, jnp.where(in_k, 0.0, row_j))
            row_k = jnp.where(in_k, 1.0, jnp.where(in_j, 0.0, row_k)) - (b * over_a) * row_j
            for h in range(g, BLOCK // 8):
                if h > g:
                    x, y = lanes(groups[h], j), lanes(groups[h], j + 1)
                u = x * over_a
                v = (a * y - b * x) * over_det
                new = jnp.where(pivots, 0.0, groups[h]) - u * row_j - v * row_k
                if h == g:
                    new = jnp.where(sub > i + 1, new, here)
                    new = jnp.where(sub == i, row_j, jnp.where(sub == i + 1, row_k, new))
                groups[h] = new
            scale = jnp.where(sub == i, lax.rsqrt(a), scale)
            scale = jnp.where(sub == i + 1, lax.rsqrt(det * over_a), scale)
        done.append(jnp.where(sub + g * 8 >= at, groups[g] * scale, 0.0))
    packed = jnp.concatenate(done, axis=0)
    return [packed[:, :BLOCK], packed[:, BLOCK:]]


def turn(value, start):
    return pltpu.roll(value, lax.rem(RANK - start, RANK), 1)


def cholesky_kernel(pos_ref, p_ref, *refs):
    t0, t1, left_ref, x_ref, inv_ref, scr = refs[:8], refs[8:13], *refs[13:]
    rows = lax.broadcasted_iota(jnp.int32, (RANK, RANK), 0)
    cols = lax.broadcasted_iota(jnp.int32, (RANK, RANK), 1)
    z, x = pos_ref[0], pos_ref[1]
    for k in range(NZ):
        scr[0, dsm(ring_at(z, k, NZ) * 32, 32, 32), :] = t0[k][...]
    for k, ref in zip((0, 1, 3), (t1[0], t1[1], t1[4])):
        scr[1, dsm(ring_at(x, k, NX) * 64, 64, 64), :] = ref[...]
    opposite = ring_at(x, 2, NX) * 64
    scr[1, dsm(opposite, 32, 32), :] = t1[2][...]
    scr[1, dsm(opposite + 32, 32, 32), :] = t1[3][...]
    for m in range(MATS):
        scr[m] = scr[m] + jnp.where(rows == cols, EPS, 0.0)
    wide = lax.broadcasted_iota(jnp.int32, (BLOCK, RANK), 1)
    low = lax.broadcasted_iota(jnp.int32, (BLOCK, RANK), 0)
    for s in range(0, RANK, BLOCK):
        e = s + BLOCK
        inverse = invert_blocks(jnp.concatenate([scr[m, s:e, s:e] for m in range(MATS)], axis=1))
        for m in range(MATS):
            panel = scr[m, s : s + BLOCK, :]
            inside = (wide >= s) & (wide < s + BLOCK)
            panel = jnp.where(inside, jnp.where(wide == low + s, 1.0, 0.0), panel)
            panel = dot_full(inverse[m], panel)
            scr[m, s : s + BLOCK, :] = panel
            if e < RANK:
                low_edge = e // 128 * 128
                change = dot_full(panel[:, low_edge:].T, panel)
                below = jnp.where((cols[e:] >= s) & (cols[e:] < e), 0.0, scr[m, e:, :])
                scr[m, e:, :] = below - change[e - low_edge :]
    for m in range(MATS):
        inverse = jnp.where(rows >= cols, scr[m], 0.0)
        start = pos_ref[m] * (64 if m else 32)
        inv_ref[m] = turn(inverse, start)
        left = dot3(split(p_ref[m]), split(inverse.T))
        left_ref[m] = left
        x_ref[m] = turn((1.0 - KEEP) * dot3(split(left), split(inverse)), start)


CHUNK = 1024
T_ROWS = [32] * NZ, [64, 64, 32, 32, 64]


def t_specs(index):
    return [pl.BlockSpec((n, CHUNK), index[m]) for m in range(MATS) for n in T_ROWS[m]]


def stacked(refs):
    return split(jnp.concatenate([ref[...] for ref in refs], axis=0))


def right_kernel(pos_ref, inv_ref, *refs):
    t0, t1, share_ref, sq_ref, out_scr, total, flip = refs[:8], refs[8:13], *refs[13:]
    m, f = pl.program_id(0), pl.program_id(1)
    lhs = split(inv_ref[0])

    @pl.when(m == 0)
    def _():
        out_scr[...] = dot3(lhs, stacked(t0))

    @pl.when(m == 1)
    def _():
        out_scr[...] = dot3(lhs, stacked(t1))

    @pl.when(f == 0)
    def _():
        total[...] = jnp.zeros_like(total)

    for s in range(0, CHUNK, 256):
        a, b = out_scr[:, s : s + 128], out_scr[:, s + 128 : s + 256]
        total[...] += a * a + b * b

    @pl.when(f == FIELDS // CHUNK - 1)
    def _():
        sq_ref[0] = jnp.sum(total[...].T, axis=0, keepdims=True)

    first = pos_ref[0] * 256 + pos_ref[1] * 64

    @pl.when(f == first // CHUNK)
    def _():
        local = lax.rem(first, CHUNK)
        start = local // 128 * 128
        flip[...] = out_scr[:, dsm(start, 128, 128)].T
        share_ref[0] = flip[dsm(local - start, 64, 64), :]


def right_factor(pos, inverse, t):
    index = (
        lambda m, f: (0, jnp.where(m == 0, f, FIELDS // CHUNK - 1)),
        lambda m, f: (0, jnp.where(m == 0, 0, f)),
    )
    return pl.pallas_call(
        right_kernel,
        grid=(MATS, FIELDS // CHUNK),
        out_shape=[sds(MATS, 64, RANK), sds(MATS, 1, RANK)],
        in_specs=[SMEM, pl.BlockSpec((1, RANK, RANK), lambda m, f: (m, 0, 0))] + t_specs(index),
        out_specs=[
            pl.BlockSpec((1, 64, RANK), lambda m, f: (m, 0, 0)),
            pl.BlockSpec((1, 1, RANK), lambda m, f: (m, 0, 0)),
        ],
        scratch_shapes=[
            pltpu.VMEM((RANK, CHUNK), F32),
            pltpu.VMEM((RANK, 128), F32),
            pltpu.VMEM((128, RANK), F32),
        ],
        compiler_params=PARAMS,
        cost_estimate=pl.CostEstimate(flops=1 << 32, bytes_accessed=5 << 20, transcendentals=0),
    )(pos, inverse, *t)


def feedback_kernel(x_ref, grad_ref, mom_ref, *refs):
    t, out_ref = refs[:-1], refs[-1]
    out = dot3(split(x_ref[0]), stacked(t))
    out_ref[0] = mom_ref[0] + grad_ref[0].astype(F32) - out


def feedback_second(x_ref, grad_ref, mom_ref, *refs):
    feedback_kernel(x_ref, grad_ref, mom_ref, *refs[:-2], refs[-1])


def feedback(m, weights, gradient, momentum, t, before=()):
    block = pl.BlockSpec((1, ROWS, CHUNK), lambda f: (m, 0, f))
    return pl.pallas_call(
        feedback_second if before else feedback_kernel,
        grid=(FIELDS // CHUNK,),
        out_shape=sds(MATS, ROWS, FIELDS),
        in_specs=[pl.BlockSpec((1, RANK, RANK), lambda f: (m, 0, 0)), block, block]
        + [pl.BlockSpec((n, CHUNK), lambda f: (0, f)) for n in T_ROWS[m]]
        + [pl.BlockSpec(memory_space=pl.ANY)] * len(before),
        out_specs=block,
        input_output_aliases={3 + len(t): 0} if before else {},
        compiler_params=PARAMS,
        cost_estimate=pl.CostEstimate(flops=1 << 31, bytes_accessed=7 << 20, transcendentals=0),
    )(weights, gradient, momentum, *t, *before)


def flatten(parts):
    flat = []
    for part in parts:
        flat.extend(part if isinstance(part, tuple) else [part])
    return flat


def pair(parts, half):
    return parts[:half] + [(parts[half], parts[half + 1])] + parts[half + 2 :]


def per_device(gradient, momentum, prior_input_frame):
    row, col = lax.axis_index("row"), lax.axis_index("col")
    x_at = row % NX
    pos = jnp.stack([row // NX, x_at, col // 2, col % 2]).astype(jnp.int32)
    q = prior_input_frame[:, 0]

    q0, q1 = gather_x(pos, q[0], q[1])
    q1 = exchange(q1, "row", Z_GROUPS).reshape(NZ * 64, RANK)
    q0 = ring_gather_whole(q0, NZ, send_z)
    q1 = flatten(ring_gather(q1, NX, send_x))

    mine, other = call(
        product_kernel,
        [pos, gradient, momentum] + q0 + q1,
        [sds(NY, MATS, 32, RANK)] * 2,
        [pltpu.VMEM((MATS, FIELDS, RANK), F32), pltpu.VMEM((MATS, ROWS, RANK), F32)],
        flops=6 * MATS * ROWS * FIELDS * RANK,
        nbytes=11 << 20,
    )
    other = send_core(other)
    mine = [mine[k] + other[k] for k in range(NY)]
    share = mine[0] + sum(send_y(mine[k], k) for k in range(1, NY))
    mine = jnp.stack([share] + [send_y(share, -k) for k in range(1, NY)])
    other = send_core(mine)
    sizes0, sizes1 = [32] * 8, [64, 64, 32, 32, 64]
    product, *parts = call(
        transposed_kernel,
        [pos, mine, other, gradient, momentum],
        [sds(MATS, ROWS, RANK)] + [sds(n, WIDE) for n in sizes0 + sizes1],
        [pltpu.VMEM((RANK, ROWS), F32), pltpu.VMEM((MATS, RANK, ROWS), F32)],
        flops=6 * MATS * ROWS * FIELDS * RANK,
        nbytes=11 << 20,
    )
    share0 = ring_scatter_whole(list(parts[:8]), NZ, send_z)
    share1 = ring_scatter(pair(list(parts[8:]), 2), NX, send_x)
    pieces = [share0[k * 8 : k * 8 + 8] for k in range(NX)]
    share0 = pieces[0] + sum(send_x(pieces[k], k) for k in range(1, NX))
    share1 = jnp.sum(exchange(share1.reshape(NZ, 8, WIDE), "row", Z_GROUPS), axis=0)
    t1 = flatten(ring_gather(gather_z(share1), NX, send_x))
    t0 = ring_gather_whole(gather_x(pos, share0), NZ, send_z)
    left_basis, weights, inverse = pl.pallas_call(
        cholesky_kernel,
        grid=(1,),
        out_shape=[sds(MATS, ROWS, RANK)] * 3,
        in_specs=[SMEM, VMEM]
        + [pl.BlockSpec((n, RANK), lambda k: (0, FIELDS // RANK)) for m in range(MATS) for n in T_ROWS[m]],
        out_specs=[VMEM] * 3,
        scratch_shapes=[pltpu.VMEM((MATS, RANK, RANK), F32)],
        compiler_params=PARAMS,
        cost_estimate=pl.CostEstimate(flops=1 << 34, bytes_accessed=2 << 20, transcendentals=0),
    )(pos, product, *t0, *t1)
    share, squares = right_factor(pos, inverse, t0 + t1)
    squares = squares[:, 0]
    momentum_next = feedback(0, weights, gradient, momentum, t0)
    total = squares + sum(send_y(squares, k) for k in range(1, NY))
    total = total + send_core(total)
    momentum_next = feedback(1, weights, gradient, momentum, t1, (momentum_next,))
    fresh = share * lax.rsqrt(total / FF_WIN + EPS)[:, None]
    return momentum_next, left_basis, fresh[:, None]


def solution(mesh):
    return jax.shard_map(
        per_device,
        mesh=mesh,
        in_specs=(P(None, "row", "col"), P(None, "row", "col"), P(None, "col", "row", None)),
        out_specs=(P(None, "row", "col"), P(None, "row", None), P(None, "col", "row", None)),
        check_vma=False,
    )
```

```python
import jax
import jax.numpy as jnp
from jax import lax
from jax.experimental import pallas as pl
from jax.experimental.pallas import tpu as pltpu
from jax.sharding import PartitionSpec as P

FF_WIN = 16384
MATS = 2
ROWS = 256
FIELDS = 2048
WIDE = 2304
RANK = 256
NZ, NX, NY = 8, 4, 4
KEEP = 0.95
EPS = 1e-06
F32 = jnp.float32
BF16 = jnp.bfloat16
VMEM = pl.BlockSpec(memory_space=pltpu.VMEM)
SMEM = pl.BlockSpec(memory_space=pltpu.SMEM)
PARAMS = pltpu.CompilerParams(vmem_limit_bytes=24 * 1024 * 1024)


def sds(*shape):
    return jax.ShapeDtypeStruct(shape, F32)


def call(body, ins, outs, scratch=(), flops=0, nbytes=0):
    return pl.pallas_call(
        body,
        out_shape=outs,
        in_specs=[SMEM] + [VMEM] * (len(ins) - 1),
        out_specs=[VMEM] * len(outs),
        scratch_shapes=list(scratch),
        compiler_params=PARAMS,
        cost_estimate=pl.CostEstimate(flops=flops, bytes_accessed=nbytes, transcendentals=0),
    )(*ins)


def send_row(value, dz, dx):
    pairs = [
        (z * NX + x, (z + dz) % NZ * NX + (x + dx) % NX) for z in range(NZ) for x in range(NX)
    ]
    return lax.ppermute(value, "row", pairs)


def send_z(value, step):
    return send_row(value, step, 0)


def send_x(value, step):
    return send_row(value, 0, step)


def send_y(value, step):
    pairs = [(y * 2 + c, (y + step) % NY * 2 + c) for y in range(NY) for c in range(2)]
    return lax.ppermute(value, "col", pairs)


def send_core(value):
    return lax.ppermute(value, "col", [(k, k ^ 1) for k in range(2 * NY)])


def ring_gather_whole(value, size, send):
    got = {0: value}
    ahead = behind = value
    for k in range(1, size // 2 + 1):
        ahead = send(ahead, 1)
        got[size - k] = ahead
        if k < size // 2:
            behind = send(behind, -1)
            got[k] = behind
    return [got[k] for k in range(size)]


def ring_scatter_whole(blocks, size, send):
    half = size // 2
    ahead, behind = send(blocks[half], 1), None
    for k in range(half - 1, 0, -1):
        ahead = send(ahead + blocks[k], 1)
        part = blocks[size - k]
        behind = send(part if behind is None else behind + part, -1)
    return blocks[0] + ahead + behind


def ring_gather(value, size, send):
    half = size // 2
    got = {0: value}
    ahead = behind = value
    for k in range(1, half):
        ahead, behind = send(ahead, 1), send(behind, -1)
        got[size - k] = ahead
        got[k] = behind
    cut = value.shape[0] // 2
    got[half] = (send(ahead[:cut], 1), send(behind[cut:], -1))
    return [got[k] for k in range(size)]


def exchange(blocks, axis, groups=None):
    return lax.all_to_all(blocks, axis, 0, 0, axis_index_groups=groups, tiled=True)


def spread(value, size, axis, groups=None):
    return exchange(jnp.broadcast_to(value[None], (size,) + value.shape), axis, groups)


Z_GROUPS = [[z * NX + x for z in range(NZ)] for x in range(NX)]


def ring_scatter(blocks, size, send):
    half = size // 2
    top, bottom = blocks[half]
    cut = top.shape[0]
    top, bottom = send(top, 1), send(bottom, -1)
    ahead, behind = blocks[half - 1], blocks[size - half + 1]
    ahead = jnp.concatenate([ahead[:cut] + top, ahead[cut:]], axis=0)
    behind = jnp.concatenate([behind[:cut], behind[cut:] + bottom], axis=0)
    for k in range(half - 1, 0, -1):
        ahead, behind = send(ahead, 1), send(behind, -1)
        if k > 1:
            ahead = ahead + blocks[k - 1]
            behind = behind + blocks[size - k + 1]
    return blocks[0] + ahead + behind


def gather_z(value):
    return spread(value, NZ, "row", Z_GROUPS).reshape(NZ * value.shape[0], value.shape[1])


def split(value):
    high = value.astype(BF16)
    return high, (value - high.astype(F32)).astype(BF16)


def dot(a, b):
    return jnp.dot(a, b, preferred_element_type=F32)


def dot3(a, b):
    return dot(a[0], b[0]) + (dot(a[0], b[1]) + dot(a[1], b[0]))


def dot_full(a, b):
    return jnp.dot(a, b, preferred_element_type=F32, precision=lax.Precision.HIGHEST)


def ring_at(at, k, size):
    return lax.rem(at + k, size)


def dsm(start, size, unit):
    return pl.ds(pl.multiple_of(start, unit), size)


def order_kernel(pos_ref, *refs):
    pieces, out_ref = refs[:NX], refs[NX]
    n = pieces[0].shape[0]
    for k in range(NX):
        out_ref[dsm(ring_at(pos_ref[1], k, NX) * n, n, n), :] = pieces[k][...]


def order_and_copy_kernel(pos_ref, *refs):
    order_kernel(pos_ref, *refs[:NX], refs[NX + 1])
    for k in range(NZ):
        refs[NX + 2][k] = refs[NX][...]


def gather_x(pos, value, copied=None):
    n, width = value.shape
    pieces = [value] + [send_x(value, -k) for k in range(1, NX)]
    if copied is not None:
        return call(
            order_and_copy_kernel,
            [pos] + pieces + [copied],
            [sds(NX * n, width), sds(NZ, n, width)],
            nbytes=20 * n * width,
        )
    return call(order_kernel, [pos] + pieces, [sds(NX * n, width)], nbytes=8 * n * width)[0]


def product_kernel(pos_ref, grad_ref, mom_ref, *refs):
    q0, q1, mine, other, q_scr, p_scr = refs[:8], refs[8:13], *refs[13:]
    z, x, y, c = (pos_ref[k] for k in range(4))
    for k in range(NZ):
        q_scr[0, dsm(ring_at(z, k, NZ) * 256, 256, 256), :] = q0[k][...]
    for k in range(NX):
        base = ring_at(x, k, NX) * 64
        for kz in range(NZ):
            if k == 2:
                block = q1[2 + kz // 4][pl.ds(kz % 4 * 64, 64), :]
            else:
                block = q1[k if k < 2 else 4][pl.ds(kz * 64, 64), :]
            q_scr[1, dsm(kz * 256 + base, 64, 64), :] = block
    for m in range(MATS):
        total = None
        for f in range(0, FIELDS, 512):
            b = mom_ref[m, :, f : f + 512] + grad_ref[m, :, f : f + 512].astype(F32)
            part = dot3(split(b), split(q_scr[m, f : f + 512, :]))
            total = part if total is None else total + part
        p_scr[m] = total
    for k in range(NY):
        at = ring_at(y, k, NY) * 32
        mine[k] = p_scr[:, dsm(c * 128 + at, 32, 32), :]
        other[k] = p_scr[:, dsm(128 - c * 128 + at, 32, 32), :]


def transposed_kernel(pos_ref, mine, other, grad_ref, mom_ref, p_ref, *refs):
    t0, t1, a_scr, b_scr = refs[:8], refs[8:13], *refs[13:]
    z, x = pos_ref[0], pos_ref[1]
    y, c = pos_ref[2], pos_ref[3]
    for k in range(NY):
        at = ring_at(y, k, NY) * 32
        p_ref[:, dsm(c * 128 + at, 32, 32), :] = mine[k]
        p_ref[:, dsm(128 - c * 128 + at, 32, 32), :] = other[k]
    for m in range(MATS):
        a_scr[...] = p_ref[m].T
        for kz in range(NZ):
            for kx in range(NX):
                zz, xx = ring_at(z, kz, NZ), ring_at(x, kx, NX)
                if m == 0:
                    to, at = (kz * NX + kx) * 8, (zz * NX + xx) * 8
                else:
                    to, at = (kx * NZ + kz) * 8, (xx * NZ + kz) * 8
                b_scr[m, to : to + 8, :] = a_scr[dsm(at, 8, 8), :]
        lhs = split(b_scr[m])
        for f in list(range(0, FIELDS, 512)) + [FIELDS]:
            if f < FIELDS:
                b = mom_ref[m, :, f : f + 512] + grad_ref[m, :, f : f + 512].astype(F32)
                out = dot3(lhs, split(b))
            else:
                out = dot_full(b_scr[m], p_ref[m])
            sizes = [32] * 8 if m == 0 else [64, 64, 32, 32, 64]
            at = 0
            for ref, size in zip(t0 if m == 0 else t1, sizes):
                ref[:, f : f + out.shape[1]] = out[at : at + size]
                at += size


BLOCK = 64


def invert_blocks(pair):
    shape = (8, 2 * BLOCK)
    lane = lax.broadcasted_iota(jnp.int32, shape, 1)
    sub = lax.broadcasted_iota(jnp.int32, shape, 0)
    first = lane < BLOCK
    at = lane % BLOCK

    def lanes(group, j):
        left = jnp.broadcast_to(group[:, j : j + 1], shape)
        return jnp.where(first, left, jnp.broadcast_to(group[:, BLOCK + j : BLOCK + j + 1], shape))

    groups = [pair[g : g + 8, :] for g in range(0, BLOCK, 8)]
    done = []
    for g in range(BLOCK // 8):
        scale = jnp.ones(shape, F32)
        for i in range(0, 8, 2):
            j = g * 8 + i
            here = groups[g]
            x, y = lanes(here, j), lanes(here, j + 1)
            a = jnp.broadcast_to(x[i : i + 1], shape)
            b = jnp.broadcast_to(x[i + 1 : i + 2], shape)
            c = jnp.broadcast_to(y[i + 1 : i + 2], shape)
            over_a = 1.0 / a
            det = a * c - b * b
            over_det = 1.0 / det
            row_j = jnp.broadcast_to(here[i : i + 1], shape)
            row_k = jnp.broadcast_to(here[i + 1 : i + 2], shape)
            in_j, in_k = at == j, at == j + 1
            pivots = in_j | in_k
            row_j = jnp.where(in_j, 1.0, jnp.where(in_k, 0.0, row_j))
            row_k = jnp.where(in_k, 1.0, jnp.where(in_j, 0.0, row_k)) - (b * over_a) * row_j
            for h in range(g, BLOCK // 8):
                if h > g:
                    x, y = lanes(groups[h], j), lanes(groups[h], j + 1)
                u = x * over_a
                v = (a * y - b * x) * over_det
                new = jnp.where(pivots, 0.0, groups[h]) - u * row_j - v * row_k
                if h == g:
                    new = jnp.where(sub > i + 1, new, here)
                    new = jnp.where(sub == i, row_j, jnp.where(sub == i + 1, row_k, new))
                groups[h] = new
            scale = jnp.where(sub == i, lax.rsqrt(a), scale)
            scale = jnp.where(sub == i + 1, lax.rsqrt(det * over_a), scale)
        done.append(jnp.where(sub + g * 8 >= at, groups[g] * scale, 0.0))
    packed = jnp.concatenate(done, axis=0)
    return [packed[:, :BLOCK], packed[:, BLOCK:]]


def turn(value, start):
    return pltpu.roll(value, lax.rem(RANK - start, RANK), 1)


def cholesky_kernel(pos_ref, p_ref, *refs):
    t0, t1, left_ref, x_ref, inv_ref, scr = refs[:8], refs[8:13], *refs[13:]
    rows = lax.broadcasted_iota(jnp.int32, (RANK, RANK), 0)
    cols = lax.broadcasted_iota(jnp.int32, (RANK, RANK), 1)
    z, x = pos_ref[0], pos_ref[1]
    for k in range(NZ):
        scr[0, dsm(ring_at(z, k, NZ) * 32, 32, 32), :] = t0[k][...]
    for k, ref in zip((0, 1, 3), (t1[0], t1[1], t1[4])):
        scr[1, dsm(ring_at(x, k, NX) * 64, 64, 64), :] = ref[...]
    opposite = ring_at(x, 2, NX) * 64
    scr[1, dsm(opposite, 32, 32), :] = t1[2][...]
    scr[1, dsm(opposite + 32, 32, 32), :] = t1[3][...]
    for m in range(MATS):
        scr[m] = scr[m] + jnp.where(rows == cols, EPS, 0.0)
    wide = lax.broadcasted_iota(jnp.int32, (BLOCK, RANK), 1)
    low = lax.broadcasted_iota(jnp.int32, (BLOCK, RANK), 0)
    for s in range(0, RANK, BLOCK):
        e = s + BLOCK
        inverse = invert_blocks(jnp.concatenate([scr[m, s:e, s:e] for m in range(MATS)], axis=1))
        for m in range(MATS):
            panel = scr[m, s : s + BLOCK, :]
            inside = (wide >= s) & (wide < s + BLOCK)
            panel = jnp.where(inside, jnp.where(wide == low + s, 1.0, 0.0), panel)
            panel = dot_full(inverse[m], panel)
            scr[m, s : s + BLOCK, :] = panel
            if e < RANK:
                low_edge = e // 128 * 128
                change = dot_full(panel[:, low_edge:].T, panel)
                below = jnp.where((cols[e:] >= s) & (cols[e:] < e), 0.0, scr[m, e:, :])
                scr[m, e:, :] = below - change[e - low_edge :]
    for m in range(MATS):
        inverse = jnp.where(rows >= cols, scr[m], 0.0)
        start = pos_ref[m] * (64 if m else 32)
        inv_ref[m] = turn(inverse, start)
        left = dot3(split(p_ref[m]), split(inverse.T))
        left_ref[m] = left
        x_ref[m] = turn((1.0 - KEEP) * dot3(split(left), split(inverse)), start)


CHUNK = 1024
T_ROWS = [32] * NZ, [64, 64, 32, 32, 64]


def t_specs(index):
    return [pl.BlockSpec((n, CHUNK), index[m]) for m in range(MATS) for n in T_ROWS[m]]


def stacked(refs):
    return split(jnp.concatenate([ref[...] for ref in refs], axis=0))


def right_kernel(pos_ref, inv_ref, *refs):
    t0, t1, share_ref, sq_ref, out_scr, total, flip = refs[:8], refs[8:13], *refs[13:]
    m, f = pl.program_id(0), pl.program_id(1)
    lhs = split(inv_ref[0])

    @pl.when(m == 0)
    def _():
        out_scr[...] = dot3(lhs, stacked(t0))

    @pl.when(m == 1)
    def _():
        out_scr[...] = dot3(lhs, stacked(t1))

    @pl.when(f == 0)
    def _():
        total[...] = jnp.zeros_like(total)

    for s in range(0, CHUNK, 256):
        a, b = out_scr[:, s : s + 128], out_scr[:, s + 128 : s + 256]
        total[...] += a * a + b * b

    @pl.when(f == FIELDS // CHUNK - 1)
    def _():
        sq_ref[0] = jnp.sum(total[...].T, axis=0, keepdims=True)

    first = pos_ref[0] * 256 + pos_ref[1] * 64

    @pl.when(f == first // CHUNK)
    def _():
        local = lax.rem(first, CHUNK)
        start = local // 128 * 128
        flip[...] = out_scr[:, dsm(start, 128, 128)].T
        share_ref[0] = flip[dsm(local - start, 64, 64), :]


def right_factor(pos, inverse, t):
    index = (
        lambda m, f: (0, jnp.where(m == 0, f, FIELDS // CHUNK - 1)),
        lambda m, f: (0, jnp.where(m == 0, 0, f)),
    )
    return pl.pallas_call(
        right_kernel,
        grid=(MATS, FIELDS // CHUNK),
        out_shape=[sds(MATS, 64, RANK), sds(MATS, 1, RANK)],
        in_specs=[SMEM, pl.BlockSpec((1, RANK, RANK), lambda m, f: (m, 0, 0))] + t_specs(index),
        out_specs=[
            pl.BlockSpec((1, 64, RANK), lambda m, f: (m, 0, 0)),
            pl.BlockSpec((1, 1, RANK), lambda m, f: (m, 0, 0)),
        ],
        scratch_shapes=[
            pltpu.VMEM((RANK, CHUNK), F32),
            pltpu.VMEM((RANK, 128), F32),
            pltpu.VMEM((128, RANK), F32),
        ],
        compiler_params=PARAMS,
        cost_estimate=pl.CostEstimate(flops=1 << 32, bytes_accessed=5 << 20, transcendentals=0),
    )(pos, inverse, *t)


def feedback_kernel(x_ref, grad_ref, mom_ref, *refs):
    t, out_ref = refs[:-1], refs[-1]
    out = dot3(split(x_ref[0]), stacked(t))
    out_ref[0] = mom_ref[0] + grad_ref[0].astype(F32) - out


def feedback_second(x_ref, grad_ref, mom_ref, *refs):
    feedback_kernel(x_ref, grad_ref, mom_ref, *refs[:-2], refs[-1])


def feedback(m, weights, gradient, momentum, t, before=()):
    block = pl.BlockSpec((1, ROWS, CHUNK), lambda f: (m, 0, f))
    return pl.pallas_call(
        feedback_second if before else feedback_kernel,
        grid=(FIELDS // CHUNK,),
        out_shape=sds(MATS, ROWS, FIELDS),
        in_specs=[pl.BlockSpec((1, RANK, RANK), lambda f: (m, 0, 0)), block, block]
        + [pl.BlockSpec((n, CHUNK), lambda f: (0, f)) for n in T_ROWS[m]]
        + [pl.BlockSpec(memory_space=pl.ANY)] * len(before),
        out_specs=block,
        input_output_aliases={3 + len(t): 0} if before else {},
        compiler_params=PARAMS,
        cost_estimate=pl.CostEstimate(flops=1 << 31, bytes_accessed=7 << 20, transcendentals=0),
    )(weights, gradient, momentum, *t, *before)


def flatten(parts):
    flat = []
    for part in parts:
        flat.extend(part if isinstance(part, tuple) else [part])
    return flat


def pair(parts, half):
    return parts[:half] + [(parts[half], parts[half + 1])] + parts[half + 2 :]


def per_device(gradient, momentum, prior_input_frame):
    row, col = lax.axis_index("row"), lax.axis_index("col")
    x_at = row % NX
    pos = jnp.stack([row // NX, x_at, col // 2, col % 2]).astype(jnp.int32)
    q = prior_input_frame[:, 0]

    q1 = gather_z(q[1])
    q0 = gather_x(pos, q[0])
    q0 = ring_gather_whole(q0, NZ, send_z)
    q1 = flatten(ring_gather(q1, NX, send_x))

    mine, other = call(
        product_kernel,
        [pos, gradient, momentum] + q0 + q1,
        [sds(NY, MATS, 32, RANK)] * 2,
        [pltpu.VMEM((MATS, FIELDS, RANK), F32), pltpu.VMEM((MATS, ROWS, RANK), F32)],
        flops=6 * MATS * ROWS * FIELDS * RANK,
        nbytes=11 << 20,
    )
    other = send_core(other)
    mine = [mine[k] + other[k] for k in range(NY)]
    share = mine[0] + sum(send_y(mine[k], k) for k in range(1, NY))
    mine = jnp.stack([share] + [send_y(share, -k) for k in range(1, NY)])
    other = send_core(mine)
    sizes0, sizes1 = [32] * 8, [64, 64, 32, 32, 64]
    product, *parts = call(
        transposed_kernel,
        [pos, mine, other, gradient, momentum],
        [sds(MATS, ROWS, RANK)] + [sds(n, WIDE) for n in sizes0 + sizes1],
        [pltpu.VMEM((RANK, ROWS), F32), pltpu.VMEM((MATS, RANK, ROWS), F32)],
        flops=6 * MATS * ROWS * FIELDS * RANK,
        nbytes=11 << 20,
    )
    share0 = ring_scatter_whole(list(parts[:8]), NZ, send_z)
    share1 = ring_scatter(pair(list(parts[8:]), 2), NX, send_x)
    pieces = [share0[k * 8 : k * 8 + 8] for k in range(NX)]
    share0 = pieces[0] + sum(send_x(pieces[k], k) for k in range(1, NX))
    share1 = jnp.sum(exchange(share1.reshape(NZ, 8, WIDE), "row", Z_GROUPS), axis=0)
    t1 = flatten(ring_gather(gather_z(share1), NX, send_x))
    t0 = ring_gather_whole(gather_x(pos, share0), NZ, send_z)
    left_basis, weights, inverse = pl.pallas_call(
        cholesky_kernel,
        grid=(1,),
        out_shape=[sds(MATS, ROWS, RANK)] * 3,
        in_specs=[SMEM, VMEM]
        + [pl.BlockSpec((n, RANK), lambda k: (0, FIELDS // RANK)) for m in range(MATS) for n in T_ROWS[m]],
        out_specs=[VMEM] * 3,
        scratch_shapes=[pltpu.VMEM((MATS, RANK, RANK), F32)],
        compiler_params=PARAMS,
        cost_estimate=pl.CostEstimate(flops=1 << 34, bytes_accessed=2 << 20, transcendentals=0),
    )(pos, product, *t0, *t1)
    share, squares = right_factor(pos, inverse, t0 + t1)
    squares = squares[:, 0]
    momentum_next = feedback(0, weights, gradient, momentum, t0)
    total = squares + sum(send_y(squares, k) for k in range(1, NY))
    total = total + send_core(total)
    momentum_next = feedback(1, weights, gradient, momentum, t1, (momentum_next,))
    fresh = share * lax.rsqrt(total / FF_WIN + EPS)[:, None]
    return momentum_next, left_basis, fresh[:, None]


def solution(mesh):
    return jax.shard_map(
        per_device,
        mesh=mesh,
        in_specs=(P(None, "row", "col"), P(None, "row", "col"), P(None, "col", "row", None)),
        out_specs=(P(None, "row", "col"), P(None, "row", None), P(None, "col", "row", None)),
        check_vma=False,
    )
```
